512 devices in a mesh: dp: 128 (over y, z_lo, x), seq: 4 (over z_hi, core).
Axes of the slice: x: 4, y: 8, z: 8 (z_hi: 2, z_lo: 4; z = z_hi * 4 + z_lo), core: 2. Of those that a mesh axis runs over, the one named last changes fastest.
Arguments:
- queries: bfloat16 [128, 512, 4096], P('dp', 'seq'), may hold values from -240 to 240
- encodings: bfloat16 [128, 8, 256, 448], P('dp', 'seq'), may hold values from -6 to 6
- neighbour_ids: int32 [128, 8, 256], P('dp', 'seq'), may hold values from 0 to 31999, as said below
- w_key: bfloat16 [448, 4096], P(None, 'dp'), may hold values from -0.25 to 0.25
- w_value: bfloat16 [448, 4096], P(None, 'dp'), may hold values from -0.25 to 0.25
- cotangent: bfloat16 [128, 512, 4096], P('dp', 'seq'), may hold values from -6 to 6
Outputs:
- attended: bfloat16 [128, 512, 4096], P('dp', 'seq')
- query_grad: bfloat16 [128, 512, 4096], P('dp', 'seq')
The draws below stay inside these ranges and needn't reach their ends.
Inputs may be any that keep to these rules, and one draw needn't show every extreme that they name: `neighbour_ids`: 0 marks padding: each of the 2 neighbours of a block holds its real token ids (1 or more) first, at least 32 of them, and zeros after them.
All inputs are finite; a program needn't handle non-finite values.
Results may differ from the reference program's by a relative error of at most 0.023.
The reference program's roundings to bfloat16 on the way (of `probs_low` and `dscores`) count: a program that leaves them out, or rounds other values in their place, can miss the bound.
Values may be sent and summed in bfloat16 or wider, within the bound.
A program may use at most 128 MiB of HBM per device.

```python
import jax
import jax.numpy as jnp
from jax import lax

HD = 128
ENC = 448
BLOCK = 64
NEI = 2
NLEN = 128
VOCAB = 32000
HW = 4096
NROWS = 256
SEQ_BLOCKS = 8
SEQLEN = 512
BATCH = 128


def draw_queries(key, part):
    key = jax.random.fold_in(key, 11)
    first, second = jax.random.split(key)
    lowest, highest = (0.5, 2.0)
    logs = jax.random.uniform(first, (BATCH, SEQLEN, 1), jnp.float32, jnp.log(lowest), jnp.log(highest))
    base = jnp.clip(jax.random.normal(second, (BATCH, SEQLEN, HW), jnp.float32), -4.0, 4.0)
    return (base * jnp.exp(logs)).astype(jnp.bfloat16)


def draw_neighbour_ids(key, part):
    key = jax.random.fold_in(key, 23)
    first, second = jax.random.split(key)
    lengths = jax.random.randint(first, (BATCH, SEQ_BLOCKS, NEI, 1), NLEN // 4, NLEN + 1)
    tokens = jax.random.randint(second, (BATCH, SEQ_BLOCKS, NEI, NLEN), 1, VOCAB)
    places = jnp.arange(NLEN, dtype=jnp.int32)
    filled = jnp.where(places < lengths, tokens, 0)
    return filled.reshape(BATCH, SEQ_BLOCKS, NEI * NLEN).astype(jnp.int32)


def steps_of(key, shape, cuts, low, largest):
    def one(axis_at, shards_of):
        heights = jax.random.uniform(jax.random.fold_in(jax.random.fold_in(key, 6), axis_at), (shards_of,), jnp.float32, low / len(cuts), largest / len(cuts))
        return jnp.repeat(jnp.exp(heights), shape[axis_at] // shards_of).reshape((-1,) + (1,) * (len(shape) - axis_at - 1))

    factor_of = one(*cuts[0])
    for cut in cuts[1:]:
        factor_of = factor_of * one(*cut)
    return factor_of


def gaussian(rng, extent, scale, reach, pieces=(), kind=jnp.bfloat16):
    gain = steps_of(rng, extent, pieces, -0.22, 0.18) if pieces else 1.0
    drawn = jax.random.normal(rng, extent, jnp.float32) * scale * gain
    return jnp.minimum(jnp.maximum(drawn, -reach), reach).astype(kind)


def setup_inputs(seed: int = 0) -> dict:
    streams_of = jax.random.split(jax.random.key(seed), 7)
    return {
        "queries": draw_queries(jax.random.fold_in(streams_of[6], 71), 0),
        "encodings": gaussian(streams_of[1], (BATCH, SEQ_BLOCKS, NROWS, ENC), 1.0, 6.0, ((0, 128), (1, 4))),
        "neighbour_ids": draw_neighbour_ids(jax.random.fold_in(streams_of[6], 71), 0),
        "w_key": gaussian(streams_of[3], (ENC, HW), ENC ** -0.5, 0.25, ((1, 128),)),
        "w_value": gaussian(streams_of[4], (ENC, HW), ENC ** -0.5, 0.25, ((1, 128),)),
        "cotangent": gaussian(streams_of[5], (BATCH, SEQLEN, HW), 1.0, 6.0, ((0, 128), (1, 4))),
    }


def cross_attend(queries, keys, values, validity, cotangent):
    groups = keys.shape[0]
    width = queries.shape[1]
    length = queries.shape[0]
    heads = width // HD
    key_count = keys.shape[1]

    def arrange(matrix):
        padded = jnp.concatenate([jnp.zeros((1, width), matrix.dtype), matrix, jnp.zeros((BLOCK - 1, width), matrix.dtype)], 0)
        return padded.reshape(groups, BLOCK, heads, HD).astype(jnp.float32)

    query_groups = arrange(queries)
    grad_groups = arrange(cotangent)
    key_heads = keys.reshape(groups, key_count, heads, HD).astype(jnp.float32)
    value_heads = values.reshape(groups, key_count, heads, HD).astype(jnp.float32)
    factor = HD ** -0.5
    scores = jnp.einsum('gqhd,gkhd->ghqk', query_groups, key_heads) * factor
    scores = jnp.where(validity[:, None, None, :], scores, -1e30)
    highest = jnp.max(scores, axis=-1, keepdims=True)
    expo = jnp.exp(scores - highest)
    probs = expo / jnp.sum(expo, axis=-1, keepdims=True)
    probs_low = probs.astype(jnp.bfloat16).astype(jnp.float32)
    attended = jnp.einsum('ghqk,gkhd->gqhd', probs_low, value_heads).astype(jnp.bfloat16)
    dprobs = jnp.einsum('gqhd,gkhd->ghqk', grad_groups, value_heads)
    rowdot = jnp.sum(probs * dprobs, axis=-1, keepdims=True)
    dscores = (probs * (dprobs - rowdot) * factor).astype(jnp.bfloat16).astype(jnp.float32)
    query_grad = jnp.einsum('ghqk,gkhd->gqhd', dscores, key_heads).astype(jnp.bfloat16)
    attended = attended.reshape(groups * BLOCK, width)[1:length + 1]
    query_grad = query_grad.reshape(groups * BLOCK, width)[1:length + 1]
    return attended, query_grad


def reference(queries, encodings, neighbour_ids, w_key, w_value, cotangent):
    def one_sequence(items):
        seq_queries, seq_codes, seq_ids, seq_grad = items
        code_rows = seq_codes.reshape(-1, ENC)
        keys = jnp.dot(code_rows, w_key, preferred_element_type=jnp.float32).astype(jnp.bfloat16)
        values = jnp.dot(code_rows, w_value, preferred_element_type=jnp.float32).astype(jnp.bfloat16)
        empty = jnp.zeros((1, NROWS, HW), jnp.bfloat16)
        keys = jnp.concatenate([empty, keys.reshape(SEQ_BLOCKS, NROWS, HW)], 0)
        values = jnp.concatenate([empty, values.reshape(SEQ_BLOCKS, NROWS, HW)], 0)
        validity = jnp.concatenate([jnp.zeros((1, NROWS), bool), seq_ids != 0], 0)
        return cross_attend(seq_queries, keys, values, validity, seq_grad)

    attended, query_grad = lax.map(one_sequence, (queries, encodings, neighbour_ids, cotangent))
    return (attended, query_grad)
```

```python
import jax
import jax.numpy as jnp
from jax import lax
from jax.experimental import pallas as pl
from jax.experimental.pallas import tpu as pltpu
from jax.sharding import PartitionSpec as P

HD = 128
ENC = 448
BLOCK = 64
KEYS = 256
WIDTH = 4096
HALF = WIDTH // 2
PIECE = 32
GROUPS = 5
SHIFTED = 272
FACTOR = HD ** -0.5
EXPONENT = FACTOR * 1.4426950408889634
MASKED = -1e30
NT = (((1,), (1,)), ((), ()))
NN = (((1,), (0,)), ((), ()))
MESH = pl.DeviceIdType.MESH
GROUP_ROWS = tuple((BLOCK * g, BLOCK if g < 4 else 16) for g in range(GROUPS))
CHUNK = 32

ORDER = (
    tuple((d, i) for d in (0, 1, 3, 2) for i in range(4)),
    tuple((0, i) for i in range(4))
    + ((1, 0), (3, 0), (1, 1), (3, 1), (2, 0), (2, 1), (1, 2), (1, 3), (3, 2), (3, 3), (2, 2), (2, 3)),
)
PAIRS = (
    ((0, 0), (0, 1), (1, 0), (1, 1), (3, 0), (3, 1), (2, 0), (2, 1)),
    ((0, 0), (0, 1), (1, 0), (3, 0), (2, 0), (1, 1), (3, 1), (2, 1)),
)


def dot(a, b, dims):
    return lax.dot_general(a, b, dims, preferred_element_type=jnp.float32)


def pick(core, first, second):
    return first + core * (second - first)


def table(step, values):
    out = jnp.int32(values[0])
    for i, v in enumerate(values[1:], 1):
        out = jnp.where(step == i, jnp.int32(v), out)
    return out


def softmax_parts(s, dp, bias):
    s = s + bias
    top = jnp.max(s, axis=1, keepdims=True)
    e = jnp.exp2((s - top) * EXPONENT)
    p = e * (1.0 / jnp.sum(e, axis=1, keepdims=True))
    rowdot = jnp.sum(p * dp, axis=1, keepdims=True)
    return p.astype(jnp.bfloat16), ((p * FACTOR) * (dp - rowdot)).astype(jnp.bfloat16)


def kernel(
    q_hbm, ct_hbm, e_hbm, ids_hbm, wk_ref, wv_ref, att_hbm, gr_hbm,
    w, qraw, ctraw, qs, cts, eraw, e1, e2, ids, kb, vb, sbuf, dbuf, pbuf, dsbuf, attbuf, grbuf,
    in_sem, in_send, in_recv, prev_send, prev_recv, y_send, y_recv, a_send, a_recv, b_send, b_recv,
    f_send, f_recv, out_sem, out_send, out_recv,
):
    dp, seq = lax.axis_index("dp"), lax.axis_index("seq")
    y, zl, x = lax.div(dp, 16), lax.rem(lax.div(dp, 4), 4), lax.rem(dp, 4)
    z_hi, core = lax.div(seq, 2), lax.rem(seq, 2)
    z = z_hi * 4 + zl
    other = 1 - core
    a_me, b_me = pick(core, zl, x), pick(core, x, zl)

    def device(dy=0, dz=0, dx=0, to_core=None):
        yy, zz, xx = lax.rem(y + dy + 8, 8), lax.rem(z + dz + 8, 8), lax.rem(x + dx + 4, 4)
        return (yy * 16 + lax.rem(zz, 4) * 4 + xx, lax.div(zz, 4) * 2 + (core if to_core is None else to_core))

    def along_a(d):
        return device(dz=d * other, dx=d * core)

    def along_b(d):
        return device(dz=d * core, dx=d * other)

    sibling = device(to_core=other)

    def remote(src, dst, send, recv, to):
        return pltpu.make_async_remote_copy(
            src_ref=src, dst_ref=dst, send_sem=send, recv_sem=recv, device_id=to, device_id_type=MESH
        )

    def piece(yi, a, b):
        a, b = lax.rem(a, 4), lax.rem(b, 4)
        return w.at[pick(core, a, b) * 4 + yi, pick(core, b, a)]

    barrier = pltpu.get_barrier_semaphore()
    peers = [device(dy=d) for d in range(1, 8)] + [device(dx=d) for d in (1, 2, 3)]
    peers += [device(dz=d) for d in (1, 2, -1, -2)] + [sibling]
    peers += [device(dz=4), device(dz=4, to_core=other)]
    for peer in peers:
        pl.semaphore_signal(barrier, inc=1, device_id=peer, device_id_type=MESH)

    eye = (
        lax.broadcasted_iota(jnp.int32, (PIECE, PIECE), 0) == lax.broadcasted_iota(jnp.int32, (PIECE, PIECE), 1)
    ).astype(jnp.float32).astype(jnp.bfloat16)
    gap = jnp.zeros((512 - ENC, PIECE), jnp.bfloat16)
    left = dot(eye, jnp.concatenate([wk_ref[...], gap], 0), NT)
    right = dot(eye, jnp.concatenate([gap, wv_ref[...]], 0), NT)
    mine = w.at[zl * 4 + lax.div(y, 2), x]
    is_source = lax.rem(y, 2) == core

    @pl.when(is_source)
    def _():
        mine[:, 0:384] = left[:, 0:384].astype(jnp.bfloat16)
        mine[:, 384:512] = (left[:, 384:512] + right[:, 0:128]).astype(jnp.bfloat16)
        mine[:, 512:896] = right[:, 128:512].astype(jnp.bfloat16)

    pl.semaphore_wait(barrier, len(peers))

    def y_copy(d):
        return remote(mine, mine, y_send.at[d - 1], y_recv.at[lax.div(y, 2)], device(dy=d))

    @pl.when(is_source)
    def _():
        for d in (1, 7, 2, 6, 3, 5, 4):
            y_copy(d).start()

    def prev_copies():
        return [
            remote(
                e_hbm.at[0, 1, pl.ds(128 * t, 128)], eraw.at[0, pl.ds(128 * t, 128)],
                prev_send.at[t], prev_recv.at[0], device(dz=4, to_core=t),
            )
            for t in range(2)
        ] + [
            remote(ids_hbm.at[0], ids.at[0], prev_send.at[2 + t], prev_recv.at[1], device(dz=4, to_core=t))
            for t in range(2)
        ]

    gives_prev = jnp.logical_and(z_hi == 0, core == 1)

    @pl.when(gives_prev)
    def _():
        for copy in prev_copies():
            copy.start()

    rows = pl.ds(pl.multiple_of(core * 128, 128), 128)
    locals_, sends = [], []
    for n, (src, dst) in enumerate(((q_hbm, qraw), (ct_hbm, ctraw))):
        for i in range(4):
            own = pl.ds(pl.multiple_of(i * 1024 + core * 512, 512), 512)
            his = pl.ds(pl.multiple_of(i * 1024 + other * 512, 512), 512)
            to = dst.at[rows, pl.ds(i * 512, 512)]
            locals_.append(pltpu.make_async_copy(src.at[0, :, own], to, in_sem.at[n * 4 + i]))
            sends.append(remote(src.at[0, :, his], to, in_send.at[n * 4 + i], in_recv.at[n * 4 + i], sibling))
    mine_e = eraw.at[pl.ds(1 + 2 * core, 2)]
    locals_.append(pltpu.make_async_copy(e_hbm.at[0], mine_e, in_sem.at[8]))
    sends.append(remote(e_hbm.at[0], mine_e, in_send.at[8], in_recv.at[8], sibling))
    mine_ids = ids.at[1 + core]
    locals_.append(pltpu.make_async_copy(ids_hbm.at[0], mine_ids, in_sem.at[9]))
    sends.append(remote(ids_hbm.at[0], mine_ids, in_send.at[9], in_recv.at[9], sibling))
    for copy in locals_ + sends:
        copy.start()

    def in_wait(n):
        his_rows = pl.ds(pl.multiple_of(other * 128, 128), 128)
        if n < 8:
            buf = (qraw, ctraw)[n // 4]
            to = buf.at[his_rows, pl.ds((n % 4) * 512, 512)]
        elif n == 8:
            to = eraw.at[pl.ds(1 + 2 * other, 2)]
        else:
            to = ids.at[1 + other]
        locals_[n].wait()
        remote(to, to, in_send.at[n], in_recv.at[n], sibling).wait_recv()

    def shift(n, raw, out):
        for i in range(4):
            in_wait(n * 4 + i)

        def body(j, carry):
            cols = pl.ds(pl.multiple_of(j * 256, 256), 256)
            moved = pltpu.roll(raw[:, cols].astype(jnp.float32), 1, 0).astype(jnp.bfloat16)
            out[0:256, cols] = moved
            out[256:272, cols] = moved[0:16]
            return carry

        lax.fori_loop(0, 8, body, 0)

    shift(0, qraw, qs)
    shift(1, ctraw, cts)

    def a_copy(yi, d):
        here = piece(yi, a_me, b_me)
        far = 2 if yi % 2 == 0 else -2
        offset = {1: 1, 3: -1, 2: far}[d]
        return remote(here, here, a_send.at[yi * 3 + d - 1], a_recv.at[(4 - d) * 4 + yi], along_a(offset))

    def b_copy(da, yi, side):
        here = piece(yi, a_me + da, b_me)
        at = da * 4 + yi
        return remote(here, here, b_send.at[side * 16 + at], b_recv.at[side * 16 + at], along_b(1 - 2 * side))

    def entry(n):
        (d0, y0), (d1, y1) = ORDER[0][n], ORDER[1][n]
        return pick(core, d0, d1), pick(core, y0, y1)

    for yi in range(4):
        @pl.when(2 * yi + core != y)
        def _():
            here = piece(yi, a_me, b_me)
            remote(here, here, y_send.at[0], y_recv.at[yi], device(dy=1)).wait_recv()

        for d in (1, 3, 2):
            a_copy(yi, d).start()
        for side in range(2):
            b_copy(0, yi, side).start()

    r0 = lax.broadcasted_iota(jnp.int32, (ENC, 512), 0)
    r1 = lax.broadcasted_iota(jnp.int32, (ENC, 512), 1)
    place1 = (r0 == r1).astype(jnp.float32).astype(jnp.bfloat16)
    place2 = (r0 + (512 - ENC) == r1).astype(jnp.float32).astype(jnp.bfloat16)

    def pad(slot):
        block = eraw[slot]
        e1[pl.ds(slot * KEYS, KEYS), :] = dot(block, place1, NN).astype(jnp.bfloat16)
        e2[pl.ds(slot * KEYS, KEYS), :] = dot(block, place2, NN).astype(jnp.bfloat16)

    in_wait(8)
    in_wait(9)
    for slot in range(1, GROUPS):
        pad(slot)

    def a_arrived(n):
        da, yi = entry(n)
        there = piece(yi, a_me + da, b_me)
        remote(there, there, a_send.at[0], a_recv.at[da * 4 + yi], along_a(1)).wait_recv()
        for side in range(2):
            b_copy(da, yi, side).start()

    def forward(n, side):
        da, yi = entry(n)
        at = da * 4 + yi
        there = piece(yi, a_me + da, b_me + (3 if side == 0 else 1))
        half = there.at[pl.ds(16 * side, 16)]
        return there, at, remote(
            half, half, f_send.at[side * 16 + at], f_recv.at[side * 16 + at], along_b(1 - 2 * side)
        )

    def pass_on(first, last):
        for n in range(first, last):
            for side in range(2):
                there, at, copy = forward(n, side)
                remote(there, there, b_send.at[0], b_recv.at[side * 16 + at], along_b(1)).wait_recv()
                copy.start()

    def passed(first, last):
        for n in range(first, last):
            da, yi = entry(n)
            at = da * 4 + yi
            there = piece(yi, a_me + da, b_me + 2)
            for side in range(2):
                half = there.at[pl.ds(16 * side, 16)]
                remote(half, half, f_send.at[0], f_recv.at[side * 16 + at], along_b(1)).wait_recv()

    for n in range(4, 8):
        a_arrived(n)
    pass_on(0, 4)

    def prev_on():
        half = eraw.at[0, pl.ds(pl.multiple_of(core * 128, 128), 128)]
        return remote(half, half, prev_send.at[4], prev_recv.at[2], sibling)

    @pl.when(z_hi == 1)
    def _():
        half = eraw.at[0, pl.ds(pl.multiple_of(core * 128, 128), 128)]
        remote(half, half, prev_send.at[0], prev_recv.at[0], sibling).wait_recv()
        remote(ids.at[0], ids.at[0], prev_send.at[2], prev_recv.at[1], sibling).wait_recv()
        prev_on().start()

    @pl.when(z_hi == 0)
    def _():
        eraw[0] = jnp.zeros((KEYS, ENC), jnp.bfloat16)
        ids[0] = jnp.zeros((2, KEYS), jnp.int32)

    for n in range(8, 16):
        a_arrived(n)

    @pl.when(z_hi == 1)
    def _():
        half = eraw.at[0, pl.ds(pl.multiple_of(other * 128, 128), 128)]
        remote(half, half, prev_send.at[4], prev_recv.at[2], sibling).wait_recv()

    pad(0)

    def out_copies(step, head, col, out_col):
        found = []
        for n, (buf, out) in enumerate(((attbuf, att_hbm), (grbuf, gr_hbm))):
            at = (step * 2 + head) * 2 + n
            src = buf.at[pl.ds(pl.multiple_of(other * 128, 128), 128), col]
            found.append(remote(src, out.at[:, out_col], out_send.at[at], out_recv.at[at], sibling))
            found.append(pltpu.make_async_copy(buf.at[rows, col], out.at[:, out_col], out_sem.at[at]))
        return found

    def columns(step, head, of_core):
        dz = jnp.where(of_core == 0, table(step, [p[0] for p in PAIRS[0]]), table(step, [p[0] for p in PAIRS[1]]))
        yp = jnp.where(of_core == 0, table(step, [p[1] for p in PAIRS[0]]), table(step, [p[1] for p in PAIRS[1]]))
        zz, yi = lax.rem(zl + dz, 4), yp * 2 + head
        col = pl.ds(pl.multiple_of((yi * 4 + zz) * HD, HD), HD)
        out_col = pl.ds(pl.multiple_of((yi * 8 + of_core * 4 + zz) * HD, HD), HD)
        return zz * 4 + yi, col, out_col

    def work(step, carry):
        @pl.when(step == 0)
        def _():
            passed(0, 4)

        @pl.when(step == 1)
        def _():
            pass_on(4, 8)

        @pl.when(step == 2)
        def _():
            pass_on(8, 12)
            passed(4, 8)

        @pl.when(step == 3)
        def _():
            pass_on(12, 16)

        @pl.when(step == 4)
        def _():
            passed(8, 12)

        @pl.when(step == 6)
        def _():
            passed(12, 16)

        first = columns(step, 0, core)[0]
        cols = [columns(step, h, core)[1] for h in range(2)]
        wt = w[pl.ds(first, 2)].reshape(2 * HD, 2 * ENC)
        kb[...] = dot(e1[...], wt[:, 0:512], NT).astype(jnp.bfloat16)
        vb[...] = dot(e2[...], wt[:, 384:896], NT).astype(jnp.bfloat16)
        for h in range(2):
            hs = slice(h * HD, h * HD + HD)
            for g, (r, m) in enumerate(GROUP_ROWS):
                ks = slice(KEYS * g, KEYS * g + KEYS)
                sbuf[h, r:r + m] = dot(qs[r:r + m, cols[h]], kb[ks, hs], NT)
                dbuf[h, r:r + m] = dot(cts[r:r + m, cols[h]], vb[ks, hs], NT)
        for h in range(2):
            for g, (r, m) in enumerate(GROUP_ROWS):
                bias = jnp.where(ids[(g + 1) // 2, (g + 1) % 2:(g + 1) % 2 + 1, :] != 0, 0.0, MASKED)
                for c0 in range(r, r + m, CHUNK):
                    c1 = min(c0 + CHUNK, r + m)
                    pbuf[h, c0:c1], dsbuf[h, c0:c1] = softmax_parts(sbuf[h, c0:c1], dbuf[h, c0:c1], bias)
        for h in range(2):
            hs = slice(h * HD, h * HD + HD)
            for buf, weights, other_side in ((attbuf, pbuf, vb), (grbuf, dsbuf, kb)):
                parts = [
                    dot(weights[h, r:r + m], other_side[KEYS * g:KEYS * g + KEYS, hs], NN)
                    for g, (r, m) in enumerate(GROUP_ROWS)
                ]
                moved = pltpu.roll(jnp.concatenate(parts, 0), SHIFTED - 1, 0)
                buf[:, cols[h]] = moved[0:256].astype(jnp.bfloat16)
        for h in range(2):
            _, col, out_col = columns(step, h, core)
            for copy in out_copies(step, h, col, out_col):
                copy.start()
        return carry

    lax.fori_loop(0, 8, work, 0)

    def finish(step, carry):
        for h in range(2):
            _, col, out_col = columns(step, h, core)
            _, _, his_col = columns(step, h, other)
            for n, copy in enumerate(out_copies(step, h, col, out_col)):
                if n % 2:
                    copy.wait()
                else:
                    copy.wait_send()
                    out = (att_hbm, gr_hbm)[n // 2]
                    at = (step * 2 + h) * 2 + n // 2
                    there = out.at[:, his_col]
                    remote(there, there, out_send.at[at], out_recv.at[at], sibling).wait_recv()
        return carry

    lax.fori_loop(0, 8, finish, 0)
    for copy in sends:
        copy.wait_send()

    @pl.when(is_source)
    def _():
        for d in range(1, 8):
            y_copy(d).wait_send()

    for yi in range(4):
        for d in (1, 2, 3):
            a_copy(yi, d).wait_send()
    for n in range(16):
        da, yi = entry(n)
        for side in range(2):
            b_copy(da, yi, side).wait_send()
            forward(n, side)[2].wait_send()

    @pl.when(gives_prev)
    def _():
        for copy in prev_copies():
            copy.wait_send()

    @pl.when(z_hi == 1)
    def _():
        prev_on().wait_send()


def on_device(queries, encodings, neighbour_ids, w_key, w_value, cotangent):
    bf16, f32, dma = jnp.bfloat16, jnp.float32, pltpu.SemaphoreType.DMA
    whole, anywhere = pl.BlockSpec(memory_space=pltpu.VMEM), pl.BlockSpec(memory_space=pl.ANY)
    attended, query_grad = pl.pallas_call(
        kernel,
        out_shape=(jax.ShapeDtypeStruct((128, WIDTH), bf16),) * 2,
        in_specs=[anywhere] * 4 + [whole] * 2,
        out_specs=(anywhere,) * 2,
        scratch_shapes=[
            pltpu.VMEM((16, 4, PIECE, 2 * ENC), bf16),
            pltpu.VMEM((256, HALF), bf16),
            pltpu.VMEM((256, HALF), bf16),
            pltpu.VMEM((SHIFTED, HALF), bf16),
            pltpu.VMEM((SHIFTED, HALF), bf16),
            pltpu.VMEM((GROUPS, KEYS, ENC), bf16),
            pltpu.VMEM((GROUPS * KEYS, 512), bf16),
            pltpu.VMEM((GROUPS * KEYS, 512), bf16),
            pltpu.VMEM((3, 2, KEYS), jnp.int32),
            pltpu.VMEM((GROUPS * KEYS, 2 * HD), bf16),
            pltpu.VMEM((GROUPS * KEYS, 2 * HD), bf16),
            pltpu.VMEM((2, SHIFTED, KEYS), f32),
            pltpu.VMEM((2, SHIFTED, KEYS), f32),
            pltpu.VMEM((2, SHIFTED, KEYS), bf16),
            pltpu.VMEM((2, SHIFTED, KEYS), bf16),
            pltpu.VMEM((256, HALF), bf16),
            pltpu.VMEM((256, HALF), bf16),
            dma((10,)), dma((10,)), dma((10,)),
            dma((5,)), dma((3,)),
            dma((7,)), dma((4,)),
            dma((12,)), dma((16,)),
            dma((32,)), dma((32,)),
            dma((32,)), dma((32,)),
            dma((32,)), dma((32,)), dma((32,)),
        ],
        compiler_params=pltpu.CompilerParams(
            collective_id=0, has_side_effects=True, vmem_limit_bytes=40 << 20
        ),
    )(queries, cotangent, encodings, neighbour_ids, w_key, w_value)
    return attended[None], query_grad[None]


def solution(mesh):
    return jax.shard_map(
        on_device,
        mesh=mesh,
        in_specs=(
            P("dp", "seq", None),
            P("dp", "seq", None, None),
            P("dp", "seq", None),
            P(None, "dp"),
            P(None, "dp"),
            P("dp", "seq", None),
        ),
        out_specs=(P("dp", "seq", None), P("dp", "seq", None)),
        check_vma=False,
    )
```

```python
import jax
import jax.numpy as jnp
from jax import lax
from jax.experimental import pallas as pl
from jax.experimental.pallas import tpu as pltpu
from jax.sharding import PartitionSpec as P

HD = 128
ENC = 448
BLOCK = 64
KEYS = 256
WIDTH = 4096
HALF = WIDTH // 2
PIECE = 32
GROUPS = 5
SHIFTED = 272
FACTOR = HD ** -0.5
EXPONENT = FACTOR * 1.4426950408889634
MASKED = -1e30
NT = (((1,), (1,)), ((), ()))
NN = (((1,), (0,)), ((), ()))
TN = (((0,), (0,)), ((), ()))
MESH = pl.DeviceIdType.MESH
GROUP_ROWS = tuple((BLOCK * g, BLOCK if g < 4 else 16) for g in range(GROUPS))
CHUNK = 32

ROWS = (0, 1, -1, -2, 2, 3, -3, 4)


def dot(a, b, dims):
    return lax.dot_general(a, b, dims, preferred_element_type=jnp.float32)


def pick(core, first, second):
    return first + core * (second - first)


def softmax_parts(s, dp, bias):
    s = s + bias
    top = jnp.max(s, axis=1, keepdims=True)
    e = jnp.exp2((s - top) * EXPONENT)
    p = e * (1.0 / jnp.sum(e, axis=1, keepdims=True))
    rowdot = jnp.sum(p * dp, axis=1, keepdims=True)
    return p.astype(jnp.bfloat16), ((p * FACTOR) * (dp - rowdot)).astype(jnp.bfloat16)


def kernel(
    q_hbm, ct_hbm, e_hbm, ids_hbm, wk_ref, wv_ref, att_hbm, gr_hbm,
    w, qraw, ctraw, qs, cts, eraw, e1, e2, ids, kb, vb, sbuf, dbuf, pbuf, dsbuf, attbuf, grbuf,
    ready, in_sem, in_send, in_recv, prev_send, prev_recv, first_send, first_recv, z_send, z_recv,
    last_send, last_recv, out_sem, out_send, out_recv,
):
    dp, seq = lax.axis_index("dp"), lax.axis_index("seq")
    y, zl, x = lax.div(dp, 16), lax.rem(lax.div(dp, 4), 4), lax.rem(dp, 4)
    z_hi, core = lax.div(seq, 2), lax.rem(seq, 2)
    other = 1 - core
    zi_me = lax.div(zl, 2)
    is_source = lax.rem(zl, 2) == core
    turn = 1 - 2 * lax.rem(y, 2)
    z = z_hi * 4 + zl
    barrier = pltpu.get_barrier_semaphore()

    def place(axis, t):
        yy = lax.rem(y + t, 8) if axis == "y" else y
        zz = z_hi * 4 + lax.rem(zl + t, 4) if axis == "z" else z
        xx = lax.rem(x + t, 4) if axis == "x" else x
        return yy, zz, xx

    def peer(axis, t):
        yy, zz, xx = place(axis, t)
        return (yy * 16 + lax.rem(zz, 4) * 4 + xx, lax.div(zz, 4) * 2 + core)

    def rank(axis, yy, zz, xx):
        key = {"y": jnp.where(yy < 4, yy, 11 - yy), "x": jnp.where(xx < 2, xx, 5 - xx)}.get(axis, zz)
        return jnp.where(yy + zz + xx == 0, 99, key)

    def later(axis, t):
        return rank(axis, *place(axis, t)) > rank(axis, y, z, x)

    def slot(axis, t):
        return {"y": 0, "x": 7, "z": 10}[axis] + t - 1

    sizes = {"y": 8, "x": 4, "z": 4}
    sibling = (dp, z_hi * 2 + other)
    source1 = jnp.logical_and(is_source, core == 1)

    edges = [("z", t, True) for t in range(1, 4)] + [("x", t, core == 0) for t in (1, 3)]
    edges += [("y", t, True) for t in (1, 7)]
    gives_prev = jnp.logical_and(z_hi == 0, core == 1)
    count = 1 + jnp.where(z_hi == 1, 1, 0) + jnp.where(source1, 3, 0)

    @pl.when(source1)
    def _():
        for t in (2, 1, 3):
            pl.semaphore_signal(barrier, inc=1, device_id=peer("x", t), device_id_type=MESH)

    for axis, t, active in edges:
        after = jnp.logical_and(active, later(axis, t))
        before = jnp.logical_and(active, jnp.logical_not(later(axis, t)))
        count = count + jnp.where(before, 1, 0)

        @pl.when(after)
        def _():
            pl.semaphore_signal(barrier, inc=1, device_id=peer(axis, t), device_id_type=MESH)

    pl.semaphore_signal(barrier, inc=1, device_id=sibling, device_id_type=MESH)

    @pl.when(gives_prev)
    def _():
        for t in range(2):
            pl.semaphore_signal(barrier, inc=1, device_id=(dp, 2 + t), device_id_type=MESH)

    r0 = lax.broadcasted_iota(jnp.int32, (ENC, 512), 0)
    r1 = lax.broadcasted_iota(jnp.int32, (ENC, 512), 1)
    place1 = (r0 == r1).astype(jnp.float32).astype(jnp.bfloat16)
    place2 = (r0 + (512 - ENC) == r1).astype(jnp.float32).astype(jnp.bfloat16)
    left = dot(wk_ref[...], place1, NN)
    right = dot(wv_ref[...], place2, NN)

    def piece(zi, yy, xx):
        return w.at[lax.rem(yy + 16, 8) * 2 + zi, lax.rem(xx + 8, 4)]

    mine = piece(zi_me, y, x)

    @pl.when(is_source)
    def _():
        mine[:, 0:384] = left[:, 0:384].astype(jnp.bfloat16)
        mine[:, 384:512] = (left[:, 384:512] + right[:, 0:128]).astype(jnp.bfloat16)
        mine[:, 512:896] = right[:, 128:512].astype(jnp.bfloat16)

    def remote(src, dst, send, recv, to):
        return pltpu.make_async_remote_copy(
            src_ref=src, dst_ref=dst, send_sem=send, recv_sem=recv, device_id=to, device_id_type=MESH
        )

    def first_copy(axis, t):
        back = sizes[axis] - t
        return remote(mine, mine, first_send.at[t - 1], first_recv.at[back - 1], peer(axis, t))

    pl.semaphore_wait(barrier, count)

    @pl.when(source1)
    def _():
        for t in (2, 1, 3):
            first_copy("x", t).start()

    for axis, t, active in edges:
        before = jnp.logical_and(active, jnp.logical_not(later(axis, t)))

        @pl.when(before)
        def _():
            pl.semaphore_signal(
                ready.at[slot(axis, sizes[axis] - t)], inc=1, device_id=peer(axis, t), device_id_type=MESH
            )

    @pl.when(z_hi == 1)
    def _():
        pl.semaphore_signal(ready.at[13 + core], inc=1, device_id=(dp, 1), device_id_type=MESH)

    def ensure(axis, t):
        @pl.when(later(axis, t))
        def _():
            pl.semaphore_wait(ready.at[slot(axis, t)], 1)

    def first_wait(axis, t, there):
        remote(there, there, first_send.at[0], first_recv.at[t - 1], peer(axis, 1)).wait_recv()

    def z_copy(i, t, here):
        return remote(here, here, z_send.at[i * 3 + t - 1], z_recv.at[zi_me * 8 + i], peer("z", t))

    def z_wait(zi, i, there):
        remote(there, there, z_send.at[0], z_recv.at[zi * 8 + i], peer("z", 1)).wait_recv()

    rows = pl.ds(pl.multiple_of(core * 128, 128), 128)
    his_rows = pl.ds(pl.multiple_of(other * 128, 128), 128)

    def head_columns(zi, yy, of_core):
        return pl.ds(pl.multiple_of((yy * 4 + zi * 2 + of_core) * HD, HD), HD)

    mine_e, his_e = eraw.at[pl.ds(1 + 2 * core, 2)], eraw.at[pl.ds(1 + 2 * other, 2)]

    def whole_in(n, send_part):
        buf = (qraw, ctraw)[n]
        part = buf.at[rows if send_part else his_rows]
        return remote(part, part, in_send.at[n], in_recv.at[n], sibling)

    def exchange(n):
        src, dst = (q_hbm, qraw)[0:2] if n == 0 else (ct_hbm, ctraw)

        def body(j, carry):
            yy, zi = lax.div(j, 2), lax.rem(j, 2)
            to = dst.at[rows, pl.ds(pl.multiple_of(j * HD, HD), HD)]
            pltpu.make_async_copy(src.at[0, :, head_columns(zi, yy, core)], to, in_sem.at[n]).start()
            remote(src.at[0, :, head_columns(zi, yy, other)], to, in_send.at[n], in_recv.at[n], sibling).start()
            return carry

        lax.fori_loop(0, 16, body, 0)

    locals_ = {
        2: pltpu.make_async_copy(e_hbm.at[0], mine_e, in_sem.at[2]),
        3: pltpu.make_async_copy(ids_hbm.at[0], ids.at[1 + core], in_sem.at[3]),
    }
    sends = {
        2: remote(e_hbm.at[0], mine_e, in_send.at[2], in_recv.at[2], sibling),
        3: remote(ids_hbm.at[0], ids.at[1 + core], in_send.at[3], in_recv.at[3], sibling),
    }
    exchange(0)
    exchange(1)
    for n in (2, 3):
        locals_[n].start()
        sends[n].start()

    def in_wait(n):
        if n < 2:
            buf = (qraw, ctraw)[n]
            pltpu.make_async_copy(buf.at[rows], buf.at[rows], in_sem.at[n]).wait()
            whole_in(n, False).wait_recv()
        else:
            locals_[n].wait()
            to = his_e if n == 2 else ids.at[1 + other]
            remote(to, to, in_send.at[n], in_recv.at[n], sibling).wait_recv()

    def shift(n):
        raw, out = ((qraw, qs), (ctraw, cts))[n]
        in_wait(n)

        def body(j, carry):
            cols = pl.ds(pl.multiple_of(j * 256, 256), 256)
            moved = pltpu.roll(raw[:, cols].astype(jnp.float32), 1, 0).astype(jnp.bfloat16)
            out[0:256, cols] = moved
            out[256:272, cols] = moved[0:16]
            return carry

        lax.fori_loop(0, 8, body, 0)

    def pad(slots):
        def body(n, carry):
            block = eraw[n]
            at = pl.ds(pl.multiple_of(n * KEYS, KEYS), KEYS)
            e1[at, :] = dot(block, place1, TN).astype(jnp.bfloat16)
            e2[at, :] = dot(block, place2, TN).astype(jnp.bfloat16)
            return carry

        lax.fori_loop(slots[0], slots[1], body, 0)

    def prepare(n):
        if n < 2:
            shift(n)
        elif n == 2:
            in_wait(2)
            in_wait(3)
            pad((1, 3))
        elif n == 3:
            pad((3, 5))

    def zi_of(r):
        return zi_me if r == 0 else 1 - zi_me

    def row(i):
        return y + (4 if ROWS[i] == 4 else ROWS[i] * turn) + 8

    def along_x(r, i, side):
        here = piece(zi_of(r), row(i), x)
        at = side * 16 + r * 8 + i
        return remote(here, here, last_send.at[at], last_recv.at[at], peer("x", 1 if side == 0 else 3))

    def x_forward(r, i, side):
        there = piece(zi_of(r), row(i), x + (3 if side == 0 else 1))
        at = 32 + side * 16 + r * 8 + i
        half = there.at[pl.ds(16 * side, 16)]
        copy = remote(half, half, last_send.at[at], last_recv.at[at], peer("x", 1 if side == 0 else 3))
        return there, copy

    def x_pass_on(*numbers):
        for i, r in ((i, r) for i in numbers for r in range(2)):
            for side in range(2):
                there, copy = x_forward(r, i, side)
                at = side * 16 + r * 8 + i
                remote(there, there, last_send.at[0], last_recv.at[at], peer("x", 1)).wait_recv()
                copy.start()

    def x_passed(i):
        for r in range(2):
            there = piece(zi_of(r), row(i), x + 2)
            for side in range(2):
                half = there.at[pl.ds(16 * side, 16)]
                at = 32 + side * 16 + r * 8 + i
                remote(half, half, last_send.at[0], last_recv.at[at], peer("x", 1)).wait_recv()

    def y_side(i):
        return lax.div(1 + turn, 2) if ROWS[i] > 0 else lax.div(1 - turn, 2)

    def ring_copy(r, i, side, distance):
        here = piece(zi_of(r), row(i), x)
        if distance == 3:
            here = here.at[pl.ds(pl.multiple_of(16 * side, 16), 16)]
        at = side * 8 + distance * 2 + r
        t = 1 + 6 * side
        yy = lax.rem(y + t, 8)
        return remote(here, here, first_send.at[at], first_recv.at[at], (yy * 16 + zl * 4 + x, seq))

    def ring_wait(r, i, side, distance):
        there = piece(zi_of(r), row(i), x)
        if distance == 4:
            there = there.at[pl.ds(16 * side, 16)]
        at = side * 8 + (distance - 1) * 2 + r
        remote(there, there, first_send.at[0], first_recv.at[at], peer("y", 1)).wait_recv()

    def z_phase():
        @pl.when(is_source)
        def _():
            for t in (1, 3, 2):
                ensure("z", t)
                z_copy(0, t, mine).start()

        for r in range(2):
            if r == 0:
                pl.when(jnp.logical_not(is_source))(lambda: z_wait(zi_me, 0, mine))
            else:
                z_wait(1 - zi_me, 0, piece(1 - zi_me, y, x))
            for side in range(2):
                if r == 0:
                    ensure("y", 1 + 6 * side)
                    ensure("x", 1 + 2 * side)
                ring_copy(r, 0, side, 0).start()
                along_x(r, 0, side).start()

    def y_ring(distance):
        for i in range(1, 8):
            if abs(ROWS[i]) != distance:
                continue
            for r in range(2):
                if distance == 4:
                    ring_wait(r, i, 0, 4)
                    ring_wait(r, i, 1, 4)
                else:
                    ring_wait(r, i, y_side(i), distance)
                    ring_copy(r, i, y_side(i), distance).start()
                for side in range(2):
                    along_x(r, i, side).start()

    def along_y(r, j, side, distance):
        there = piece(zi_of(r), y + (8 - distance if side == 0 else distance) + 8, x + j)
        if distance == 3:
            there = there.at[pl.ds(16 * side, 16)]
        at = side * 32 + distance * 8 + r * 4 + j
        return remote(there, there, last_send.at[at], last_recv.at[at], peer("y", 1 if side == 0 else 7))

    def y_arrived(r, distance):
        for j in range(4):
            for side in range(2):
                there = piece(zi_of(r), y + (8 - distance if side == 0 else distance) + 8, x + j)
                if distance == 4:
                    there = there.at[pl.ds(16 * side, 16)]
                at = side * 32 + (distance - 1) * 8 + r * 4 + j
                remote(there, there, last_send.at[0], last_recv.at[at], peer("y", 1)).wait_recv()
                if distance < 4:
                    along_y(r, j, side, distance).start()

    def x_first(j):
        here = piece(zi_me, y, x + j)

        @pl.when(is_source)
        def _():
            if j:
                first_wait("x", j, here)
            for t in (1, 3, 2):
                if j == 0:
                    ensure("z", t)
                z_copy(j, t, here).start()

        @pl.when(jnp.logical_not(is_source))
        def _():
            z_wait(zi_me, j, here)

        for side in range(2):
            if j == 0:
                ensure("y", 1 if side == 0 else 7)
            along_y(0, j, side, 0).start()

    def x_second():
        for j in range(4):
            z_wait(1 - zi_me, j, piece(1 - zi_me, y, x + j))
            for side in range(2):
                along_y(1, j, side, 0).start()

    def prev_copies():
        return [
            remote(
                e_hbm.at[0, 1, pl.ds(224 * t, 224)], eraw.at[0, pl.ds(224 * t, 224)],
                prev_send.at[t], prev_recv.at[0], (dp, 2 + t),
            )
            for t in range(2)
        ] + [
            remote(ids_hbm.at[0], ids.at[0], prev_send.at[2 + t], prev_recv.at[1], (dp, 2 + t)) for t in range(2)
        ]

    @pl.when(core == 0)
    def _():
        z_phase()
        prepare(0)
        y_ring(1)
        prepare(1)
        x_pass_on(0)
        prepare(2)
        y_ring(2)
        prepare(3)
        x_pass_on(1, 2)

    @pl.when(core == 1)
    def _():
        for j in range(4):
            x_first(j)
            prepare(j)
        x_second()

        @pl.when(z_hi == 0)
        def _():
            for t in range(2):
                pl.semaphore_wait(ready.at[13 + t], 1)
            for copy in prev_copies():
                copy.start()

        y_arrived(0, 1)
        y_arrived(1, 1)

    def prev_on():
        half = eraw.at[0, pl.ds(pl.multiple_of(core * 224, 32), 224)]
        return remote(half, half, prev_send.at[4], prev_recv.at[2], sibling)

    def prev_arrived():
        half = eraw.at[0, pl.ds(pl.multiple_of(core * 224, 32), 224)]
        remote(half, half, prev_send.at[0], prev_recv.at[0], sibling).wait_recv()
        remote(ids.at[0], ids.at[0], prev_send.at[2], prev_recv.at[1], sibling).wait_recv()
        prev_on().start()

    def prev_whole():
        @pl.when(z_hi == 1)
        def _():
            half = eraw.at[0, pl.ds(pl.multiple_of(other * 224, 32), 224)]
            remote(half, half, prev_send.at[4], prev_recv.at[2], sibling).wait_recv()

        @pl.when(z_hi == 0)
        def _():
            eraw[0] = jnp.zeros((ENC, KEYS), jnp.bfloat16)
            ids[0] = jnp.zeros((2, KEYS), jnp.int32)

        pad((0, 1))

    def out_copies(step, head, col, out_col):
        found = []
        for n, (buf, out) in enumerate(((attbuf, att_hbm), (grbuf, gr_hbm))):
            at = (step * 2 + head) * 2 + n
            src = buf.at[his_rows, col]
            found.append(remote(src, out.at[:, out_col], out_send.at[at], out_recv.at[at], sibling))
            found.append(pltpu.make_async_copy(buf.at[rows, col], out.at[:, out_col], out_sem.at[at]))
        return found

    def columns(step, head, of_core):
        forth = jnp.where(jnp.logical_or(step == 0, step == 7), lax.div(step, 7) * 4, 0)
        for i in range(1, 7):
            forth = jnp.where(step == i, ROWS[i] * turn, forth)
        yy = lax.rem(y + forth + 8, 8)
        hh = yy * 2 + head
        return hh, pl.ds(pl.multiple_of(hh * HD, HD), HD), head_columns(head, yy, of_core)

    arrivals = (
        (
            lambda: None,
            lambda: (y_ring(3), x_pass_on(3, 4)),
            lambda: (y_ring(4), x_pass_on(5, 6)),
            lambda: x_pass_on(7),
        ),
        (
            lambda: None,
            lambda: y_arrived(0, 2),
            lambda: y_arrived(1, 2),
            lambda: y_arrived(0, 3),
            lambda: y_arrived(1, 3),
        ),
    )

    def work(step, carry):
        for c in range(2):
            for k, pass_on in enumerate(arrivals[c]):
                pl.when(jnp.logical_and(step == k, core == c))(lambda pass_on=pass_on: pass_on() and None)

        pl.when(jnp.logical_and(step == 0, z_hi == 1))(prev_arrived)
        turn_of = step - z_hi

        @pl.when(jnp.logical_and(turn_of >= 0, turn_of < 8))
        def _():
            attend(turn_of)

        return carry

    def attend(step):
        pl.when(step == 0)(prev_whole)
        for i in range(8):
            pl.when(jnp.logical_and(step == i, core == 0))(lambda i=i: x_passed(i))

        @pl.when(jnp.logical_and(step == 7, core == 1))
        def _():
            y_arrived(0, 4)
            y_arrived(1, 4)

        first = columns(step, 0, core)[0]
        cols = [columns(step, h, core)[1] for h in range(2)]
        wt = w[pl.ds(first, 2)].reshape(2 * HD, 2 * ENC)
        kb[...] = dot(e1[...], wt[:, 0:512], NT).astype(jnp.bfloat16)
        vb[...] = dot(e2[...], wt[:, 384:896], NT).astype(jnp.bfloat16)
        for h in range(2):
            hs = slice(h * HD, h * HD + HD)
            for g, (r, m) in enumerate(GROUP_ROWS):
                ks = slice(KEYS * g, KEYS * g + KEYS)
                sbuf[h, r:r + m] = dot(qs[r:r + m, cols[h]], kb[ks, hs], NT)
                dbuf[h, r:r + m] = dot(cts[r:r + m, cols[h]], vb[ks, hs], NT)
        for h in range(2):
            for g, (r, m) in enumerate(GROUP_ROWS):
                bias = jnp.where(ids[(g + 1) // 2, (g + 1) % 2:(g + 1) % 2 + 1, :] != 0, 0.0, MASKED)
                for c0 in range(r, r + m, CHUNK):
                    c1 = min(c0 + CHUNK, r + m)
                    pbuf[h, c0:c1], dsbuf[h, c0:c1] = softmax_parts(sbuf[h, c0:c1], dbuf[h, c0:c1], bias)
        for h in range(2):
            hs = slice(h * HD, h * HD + HD)
            for buf, weights, other_side in ((attbuf, pbuf, vb), (grbuf, dsbuf, kb)):
                parts = [
                    dot(weights[h, r:r + m], other_side[KEYS * g:KEYS * g + KEYS, hs], NN)
                    for g, (r, m) in enumerate(GROUP_ROWS)
                ]
                moved = pltpu.roll(jnp.concatenate(parts, 0), SHIFTED - 1, 0)
                buf[:, cols[h]] = moved[0:256].astype(jnp.bfloat16)
        for h in range(2):
            _, col, out_col = columns(step, h, core)
            for copy in out_copies(step, h, col, out_col):
                copy.start()

    lax.fori_loop(0, 9, work, 0)

    def finish(step, carry):
        for h in range(2):
            _, col, out_col = columns(step, h, core)
            _, _, his_col = columns(step, h, other)
            for n, copy in enumerate(out_copies(step, h, col, out_col)):
                if n % 2:
                    copy.wait()
                else:
                    copy.wait_send()
                    out = (att_hbm, gr_hbm)[n // 2]
                    at = (step * 2 + h) * 2 + n // 2
                    there = out.at[:, his_col]
                    remote(there, there, out_send.at[at], out_recv.at[at], sibling).wait_recv()
        return carry

    lax.fori_loop(0, 8, finish, 0)
    for n in range(2):
        whole_in(n, True).wait_send()
        sends[n + 2].wait_send()

    @pl.when(core == 0)
    def _():
        @pl.when(is_source)
        def _():
            for t in range(1, 4):
                z_copy(0, t, mine).wait_send()

        @pl.when(jnp.logical_not(is_source))
        def _():
            for t in range(1, 4):
                ensure("z", t)

        for r in range(2):
            for i in range(1, 7):
                ring_copy(r, i, y_side(i), abs(ROWS[i])).wait_send()
            for side in range(2):
                ring_copy(r, 0, side, 0).wait_send()

        for r in range(2):
            for i in range(8):
                for side in range(2):
                    along_x(r, i, side).wait_send()
                    x_forward(r, i, side)[1].wait_send()

    @pl.when(core == 1)
    def _():
        @pl.when(is_source)
        def _():
            for t in range(1, 4):
                first_copy("x", t).wait_send()
            for j in range(4):
                for t in range(1, 4):
                    z_copy(j, t, piece(zi_me, y, x + j)).wait_send()

        @pl.when(jnp.logical_not(is_source))
        def _():
            for t in range(1, 4):
                ensure("z", t)

        for r in range(2):
            for j in range(4):
                for side in range(2):
                    for distance in range(4):
                        along_y(r, j, side, distance).wait_send()

        @pl.when(z_hi == 0)
        def _():
            for copy in prev_copies():
                copy.wait_send()

    @pl.when(z_hi == 1)
    def _():
        prev_on().wait_send()


def on_device(queries, encodings, neighbour_ids, w_key, w_value, cotangent):
    bf16, f32, dma = jnp.bfloat16, jnp.float32, pltpu.SemaphoreType.DMA
    whole, anywhere = pl.BlockSpec(memory_space=pltpu.VMEM), pl.BlockSpec(memory_space=pl.ANY)
    attended, query_grad = pl.pallas_call(
        kernel,
        out_shape=(jax.ShapeDtypeStruct((128, WIDTH), bf16),) * 2,
        in_specs=[anywhere] * 4 + [whole] * 2,
        out_specs=(anywhere,) * 2,
        scratch_shapes=[
            pltpu.VMEM((16, 4, PIECE, 2 * ENC), bf16),
            pltpu.VMEM((256, HALF), bf16),
            pltpu.VMEM((256, HALF), bf16),
            pltpu.VMEM((SHIFTED, HALF), bf16),
            pltpu.VMEM((SHIFTED, HALF), bf16),
            pltpu.VMEM((GROUPS, ENC, KEYS), bf16),
            pltpu.VMEM((GROUPS * KEYS, 512), bf16),
            pltpu.VMEM((GROUPS * KEYS, 512), bf16),
            pltpu.VMEM((3, 2, KEYS), jnp.int32),
            pltpu.VMEM((GROUPS * KEYS, 2 * HD), bf16),
            pltpu.VMEM((GROUPS * KEYS, 2 * HD), bf16),
            pltpu.VMEM((2, SHIFTED, KEYS), f32),
            pltpu.VMEM((2, SHIFTED, KEYS), f32),
            pltpu.VMEM((2, SHIFTED, KEYS), bf16),
            pltpu.VMEM((2, SHIFTED, KEYS), bf16),
            pltpu.VMEM((256, HALF), bf16),
            pltpu.VMEM((256, HALF), bf16),
            pltpu.SemaphoreType.REGULAR((15,)),
            dma((4,)), dma((4,)), dma((4,)),
            dma((5,)), dma((3,)),
            dma((16,)), dma((16,)),
            dma((24,)), dma((16,)),
            dma((64,)), dma((64,)),
            dma((32,)), dma((32,)), dma((32,)),
        ],
        compiler_params=pltpu.CompilerParams(
            collective_id=0, has_side_effects=True, vmem_limit_bytes=60 << 20
        ),
    )(queries, cotangent, jnp.swapaxes(encodings, 2, 3), neighbour_ids, w_key.T, w_value.T)
    return attended[None], query_grad[None]


def solution(mesh):
    return jax.shard_map(
        on_device,
        mesh=mesh,
        in_specs=(
            P("dp", "seq", None),
            P("dp", "seq", None, None),
            P("dp", "seq", None),
            P(None, "dp"),
            P(None, "dp"),
            P("dp", "seq", None),
        ),
        out_specs=(P("dp", "seq", None), P("dp", "seq", None)),
        check_vma=False,
    )
```

```python
import jax
import jax.numpy as jnp
from jax import lax
from jax.experimental import pallas as pl
from jax.experimental.pallas import tpu as pltpu
from jax.sharding import PartitionSpec as P

HD = 128
ENC = 448
BLOCK = 64
KEYS = 256
WIDTH = 4096
HALF = WIDTH // 2
PIECE = 32
GROUPS = 5
SHIFTED = 272
FACTOR = HD ** -0.5
EXPONENT = FACTOR * 1.4426950408889634
MASKED = -1e30
NT = (((1,), (1,)), ((), ()))
NN = (((1,), (0,)), ((), ()))
TN = (((0,), (0,)), ((), ()))
MESH = pl.DeviceIdType.MESH
GROUP_ROWS = tuple((BLOCK * g, BLOCK if g < 4 else 16) for g in range(GROUPS))
CHUNK = 32

ROWS = (0, 1, -1, -2, 2, 3, -3, 4)


def dot(a, b, dims):
    return lax.dot_general(a, b, dims, preferred_element_type=jnp.float32)


def pick(core, first, second):
    return first + core * (second - first)


def softmax_parts(s, dp, bias):
    s = s + bias
    top = jnp.max(s, axis=1, keepdims=True)
    e = jnp.exp2((s - top) * EXPONENT)
    p = e * (1.0 / jnp.sum(e, axis=1, keepdims=True))
    rowdot = jnp.sum(p * dp, axis=1, keepdims=True)
    return p.astype(jnp.bfloat16), ((p * FACTOR) * (dp - rowdot)).astype(jnp.bfloat16)


def kernel(
    q_hbm, ct_hbm, e_hbm, ids_hbm, wk_ref, wv_ref, att_hbm, gr_hbm,
    w, qraw, ctraw, qs, cts, eraw, e1, e2, ids, kb, vb, sbuf, dbuf, pbuf, dsbuf, attbuf, grbuf,
    ready, in_sem, in_send, in_recv, prev_send, prev_recv, first_send, first_recv, z_send, z_recv,
    last_send, last_recv, out_sem, out_send, out_recv,
):
    dp, seq = lax.axis_index("dp"), lax.axis_index("seq")
    y, zl, x = lax.div(dp, 16), lax.rem(lax.div(dp, 4), 4), lax.rem(dp, 4)
    z_hi, core = lax.div(seq, 2), lax.rem(seq, 2)
    other = 1 - core
    zi_me = lax.div(zl, 2)
    is_source = lax.rem(zl, 2) == core
    turn = 1 - 2 * lax.rem(y, 2)
    z = z_hi * 4 + zl
    barrier = pltpu.get_barrier_semaphore()

    def place(axis, t):
        yy = lax.rem(y + t, 8) if axis == "y" else y
        zz = z_hi * 4 + lax.rem(zl + t, 4) if axis == "z" else z
        xx = lax.rem(x + t, 4) if axis == "x" else x
        return yy, zz, xx

    def peer(axis, t):
        yy, zz, xx = place(axis, t)
        return (yy * 16 + lax.rem(zz, 4) * 4 + xx, lax.div(zz, 4) * 2 + core)

    def rank(axis, yy, zz, xx):
        key = {"y": jnp.where(yy < 4, yy, 11 - yy), "x": jnp.where(xx < 2, xx, 5 - xx)}.get(axis, zz)
        return jnp.where(yy + zz + xx == 0, 99, key)

    def later(axis, t):
        return rank(axis, *place(axis, t)) > rank(axis, y, z, x)

    def slot(axis, t):
        return {"y": 0, "x": 7, "z": 10}[axis] + t - 1

    sizes = {"y": 8, "x": 4, "z": 4}
    sibling = (dp, z_hi * 2 + other)

    edges = [("z", t, True) for t in range(1, 4)] + [("x", t, True) for t in (1, 3)] + [("x", 2, core == 1)]
    edges += [("y", t, True) for t in (1, 7)]
    gives_prev = jnp.logical_and(z_hi == 0, core == 1)
    count = 1 + jnp.where(z_hi == 1, 1, 0)

    for axis, t, active in edges:
        after = jnp.logical_and(active, later(axis, t))
        before = jnp.logical_and(active, jnp.logical_not(later(axis, t)))
        count = count + jnp.where(before, 1, 0)

        @pl.when(after)
        def _():
            pl.semaphore_signal(barrier, inc=1, device_id=peer(axis, t), device_id_type=MESH)

    pl.semaphore_signal(barrier, inc=1, device_id=sibling, device_id_type=MESH)

    @pl.when(gives_prev)
    def _():
        for t in range(2):
            pl.semaphore_signal(barrier, inc=1, device_id=(dp, 2 + t), device_id_type=MESH)

    r0 = lax.broadcasted_iota(jnp.int32, (ENC, 512), 0)
    r1 = lax.broadcasted_iota(jnp.int32, (ENC, 512), 1)
    place1 = (r0 == r1).astype(jnp.float32).astype(jnp.bfloat16)
    place2 = (r0 + (512 - ENC) == r1).astype(jnp.float32).astype(jnp.bfloat16)
    left = dot(wk_ref[...], place1, NN)
    right = dot(wv_ref[...], place2, NN)

    def piece(zi, yy, xx):
        return w.at[lax.rem(yy + 16, 8) * 2 + zi, lax.rem(xx + 8, 4)]

    mine = piece(zi_me, y, x)

    @pl.when(is_source)
    def _():
        mine[:, 0:384] = left[:, 0:384].astype(jnp.bfloat16)
        mine[:, 384:512] = (left[:, 384:512] + right[:, 0:128]).astype(jnp.bfloat16)
        mine[:, 512:896] = right[:, 128:512].astype(jnp.bfloat16)

    def remote(src, dst, send, recv, to):
        return pltpu.make_async_remote_copy(
            src_ref=src, dst_ref=dst, send_sem=send, recv_sem=recv, device_id=to, device_id_type=MESH
        )

    pl.semaphore_wait(barrier, count)

    for axis, t, active in edges:
        before = jnp.logical_and(active, jnp.logical_not(later(axis, t)))

        @pl.when(before)
        def _():
            pl.semaphore_signal(
                ready.at[slot(axis, sizes[axis] - t)], inc=1, device_id=peer(axis, t), device_id_type=MESH
            )

    @pl.when(z_hi == 1)
    def _():
        pl.semaphore_signal(ready.at[13 + core], inc=1, device_id=(dp, 1), device_id_type=MESH)

    def ensure(axis, t):
        @pl.when(later(axis, t))
        def _():
            pl.semaphore_wait(ready.at[slot(axis, t)], 1)

    def z_copy(i, t, here):
        return remote(here, here, z_send.at[i * 3 + t - 1], z_recv.at[zi_me * 8 + i], peer("z", t))

    def z_wait(zi, i, there):
        remote(there, there, z_send.at[0], z_recv.at[zi * 8 + i], peer("z", 1)).wait_recv()

    rows = pl.ds(pl.multiple_of(core * 128, 128), 128)
    his_rows = pl.ds(pl.multiple_of(other * 128, 128), 128)

    def head_columns(zi, yy, of_core):
        return pl.ds(pl.multiple_of((yy * 4 + zi * 2 + of_core) * HD, HD), HD)

    mine_e, his_e = eraw.at[pl.ds(1 + 2 * core, 2)], eraw.at[pl.ds(1 + 2 * other, 2)]

    def whole_in(n, send_part):
        buf = (qraw, ctraw)[n]
        part = buf.at[rows if send_part else his_rows]
        return remote(part, part, in_send.at[n], in_recv.at[n], sibling)

    def exchange(n):
        src, dst = (q_hbm, qraw)[0:2] if n == 0 else (ct_hbm, ctraw)

        def body(j, carry):
            yy, zi = lax.div(j, 2), lax.rem(j, 2)
            to = dst.at[rows, pl.ds(pl.multiple_of(j * HD, HD), HD)]
            pltpu.make_async_copy(src.at[0, :, head_columns(zi, yy, core)], to, in_sem.at[n]).start()
            remote(src.at[0, :, head_columns(zi, yy, other)], to, in_send.at[n], in_recv.at[n], sibling).start()
            return carry

        lax.fori_loop(0, 16, body, 0)

    locals_ = {
        2: pltpu.make_async_copy(e_hbm.at[0], mine_e, in_sem.at[2]),
        3: pltpu.make_async_copy(ids_hbm.at[0], ids.at[1 + core], in_sem.at[3]),
    }
    sends = {
        2: remote(e_hbm.at[0], mine_e, in_send.at[2], in_recv.at[2], sibling),
        3: remote(ids_hbm.at[0], ids.at[1 + core], in_send.at[3], in_recv.at[3], sibling),
    }
    exchange(0)
    exchange(1)
    for n in (2, 3):
        locals_[n].start()
        sends[n].start()

    def in_wait(n):
        if n < 2:
            buf = (qraw, ctraw)[n]
            pltpu.make_async_copy(buf.at[rows], buf.at[rows], in_sem.at[n]).wait()
            whole_in(n, False).wait_recv()
        else:
            locals_[n].wait()
            to = his_e if n == 2 else ids.at[1 + other]
            remote(to, to, in_send.at[n], in_recv.at[n], sibling).wait_recv()

    def shift(n):
        raw, out = ((qraw, qs), (ctraw, cts))[n]
        in_wait(n)

        def body(j, carry):
            cols = pl.ds(pl.multiple_of(j * 256, 256), 256)
            moved = pltpu.roll(raw[:, cols].astype(jnp.float32), 1, 0).astype(jnp.bfloat16)
            out[0:256, cols] = moved
            out[256:272, cols] = moved[0:16]
            return carry

        lax.fori_loop(0, 8, body, 0)

    def pad(slots):
        def body(n, carry):
            block = eraw[n]
            at = pl.ds(pl.multiple_of(n * KEYS, KEYS), KEYS)
            e1[at, :] = dot(block, place1, TN).astype(jnp.bfloat16)
            e2[at, :] = dot(block, place2, TN).astype(jnp.bfloat16)
            return carry

        lax.fori_loop(slots[0], slots[1], body, 0)

    def prepare(n):
        if n < 2:
            shift(n)
        elif n == 2:
            in_wait(2)
            in_wait(3)
            pad((1, 3))
        elif n == 3:
            pad((3, 5))

    def zi_of(r):
        return zi_me if r == 0 else 1 - zi_me

    def row(i):
        return y + (4 if ROWS[i] == 4 else ROWS[i] * turn) + 8

    def along_x(r, i, side):
        here = piece(zi_of(r), row(i), x)
        at = side * 16 + r * 8 + i
        return remote(here, here, last_send.at[at], last_recv.at[at], peer("x", 1 if side == 0 else 3))

    def x_forward(r, i, side):
        there = piece(zi_of(r), row(i), x + (3 if side == 0 else 1))
        at = 32 + side * 16 + r * 8 + i
        half = there.at[pl.ds(16 * side, 16)]
        copy = remote(half, half, last_send.at[at], last_recv.at[at], peer("x", 1 if side == 0 else 3))
        return there, copy

    def x_pass_on(*numbers):
        for i, r in ((i, r) for i in numbers for r in range(2)):
            for side in range(2):
                there, copy = x_forward(r, i, side)
                at = side * 16 + r * 8 + i
                remote(there, there, last_send.at[0], last_recv.at[at], peer("x", 1)).wait_recv()
                copy.start()

    def x_passed(i):
        for r in range(2):
            there = piece(zi_of(r), row(i), x + 2)
            for side in range(2):
                half = there.at[pl.ds(16 * side, 16)]
                at = 32 + side * 16 + r * 8 + i
                remote(half, half, last_send.at[0], last_recv.at[at], peer("x", 1)).wait_recv()

    def y_side(i):
        return lax.div(1 + turn, 2) if ROWS[i] > 0 else lax.div(1 - turn, 2)

    def ring_copy(r, i, side, distance):
        here = piece(zi_of(r), row(i), x)
        if distance == 3:
            here = here.at[pl.ds(pl.multiple_of(16 * side, 16), 16)]
        at = side * 8 + distance * 2 + r
        t = 1 + 6 * side
        yy = lax.rem(y + t, 8)
        return remote(here, here, first_send.at[at], first_recv.at[at], (yy * 16 + zl * 4 + x, seq))

    def ring_wait(r, i, side, distance):
        there = piece(zi_of(r), row(i), x)
        if distance == 4:
            there = there.at[pl.ds(16 * side, 16)]
        at = side * 8 + (distance - 1) * 2 + r
        remote(there, there, first_send.at[0], first_recv.at[at], peer("y", 1)).wait_recv()

    def z_phase(forward):
        def to_later(t):
            @pl.when(jnp.logical_and(is_source, later("z", t)))
            def _():
                pl.semaphore_wait(ready.at[slot("z", t)], 1)
                z_copy(0, t, mine).start()

        for t in (1, 2, 3):
            @pl.when(jnp.logical_and(is_source, jnp.logical_not(later("z", t))))
            def _():
                z_copy(0, t, mine).start()

        to_later(1)
        to_later(2)
        pl.when(jnp.logical_not(is_source))(lambda: z_wait(zi_me, 0, mine))
        forward(0)
        to_later(3)
        z_wait(1 - zi_me, 0, piece(1 - zi_me, y, x))
        forward(1)

    def z_forward(r):
        for side in range(2):
            if r == 0:
                ensure("y", 1 + 6 * side)
                ensure("x", 1 + 2 * side)
            ring_copy(r, 0, side, 0).start()
            along_x(r, 0, side).start()

    def y_ring(distance):
        for i in range(1, 8):
            if abs(ROWS[i]) != distance:
                continue
            for r in range(2):
                if distance == 4:
                    ring_wait(r, i, 0, 4)
                    ring_wait(r, i, 1, 4)
                else:
                    ring_wait(r, i, y_side(i), distance)
                    ring_copy(r, i, y_side(i), distance).start()
                for side in range(2):
                    along_x(r, i, side).start()

    def along_y(r, j, side, distance):
        there = piece(zi_of(r), y + (8 - distance if side == 0 else distance) + 8, x + j)
        if distance == 3:
            there = there.at[pl.ds(16 * side, 16)]
        at = side * 32 + distance * 8 + r * 4 + j
        return remote(there, there, last_send.at[at], last_recv.at[at], peer("y", 1 if side == 0 else 7))

    def y_arrived(r, distance):
        for j in range(4):
            for side in range(2):
                there = piece(zi_of(r), y + (8 - distance if side == 0 else distance) + 8, x + j)
                if distance == 4:
                    there = there.at[pl.ds(16 * side, 16)]
                at = side * 32 + (distance - 1) * 8 + r * 4 + j
                remote(there, there, last_send.at[0], last_recv.at[at], peer("y", 1)).wait_recv()
                if distance < 4:
                    along_y(r, j, side, distance).start()

    def x_copy(r, t):
        here = piece(zi_of(r), y, x)
        return remote(here, here, first_send.at[r * 3 + t - 1], first_recv.at[r * 3 + 3 - t], peer("x", t))

    def x_forward_first(r):
        for t in (2, 1, 3):
            if r == 0:
                ensure("x", t)
            x_copy(r, t).start()
        for side in range(2):
            if r == 0:
                ensure("y", 1 + 6 * side)
            along_y(r, 0, side, 0).start()

    def x_phase(r):
        for j in (1, 3, 2):
            there = piece(zi_of(r), y, x + j)
            remote(there, there, first_send.at[0], first_recv.at[r * 3 + j - 1], peer("x", 1)).wait_recv()
            for side in range(2):
                along_y(r, j, side, 0).start()

    def prev_copies():
        return [
            remote(
                e_hbm.at[0, 1, pl.ds(224 * t, 224)], eraw.at[0, pl.ds(224 * t, 224)],
                prev_send.at[t], prev_recv.at[0], (dp, 2 + t),
            )
            for t in range(2)
        ] + [
            remote(ids_hbm.at[0], ids.at[0], prev_send.at[2 + t], prev_recv.at[1], (dp, 2 + t)) for t in range(2)
        ]

    @pl.when(core == 0)
    def _():
        z_phase(z_forward)
        prepare(0)
        y_ring(1)
        prepare(1)
        x_pass_on(0)
        prepare(2)
        y_ring(2)
        prepare(3)
        x_pass_on(1, 2)

    @pl.when(core == 1)
    def _():
        z_phase(x_forward_first)
        prepare(0)
        x_phase(0)
        x_phase(1)
        for n in range(1, 4):
            prepare(n)

        @pl.when(z_hi == 0)
        def _():
            for t in range(2):
                pl.semaphore_wait(ready.at[13 + t], 1)
            for copy in prev_copies():
                copy.start()

        y_arrived(0, 1)
        y_arrived(1, 1)

    def prev_on():
        half = eraw.at[0, pl.ds(pl.multiple_of(core * 224, 32), 224)]
        return remote(half, half, prev_send.at[4], prev_recv.at[2], sibling)

    def prev_arrived():
        half = eraw.at[0, pl.ds(pl.multiple_of(core * 224, 32), 224)]
        remote(half, half, prev_send.at[0], prev_recv.at[0], sibling).wait_recv()
        remote(ids.at[0], ids.at[0], prev_send.at[2], prev_recv.at[1], sibling).wait_recv()
        prev_on().start()

    def prev_whole():
        @pl.when(z_hi == 1)
        def _():
            half = eraw.at[0, pl.ds(pl.multiple_of(other * 224, 32), 224)]
            remote(half, half, prev_send.at[4], prev_recv.at[2], sibling).wait_recv()

        @pl.when(z_hi == 0)
        def _():
            eraw[0] = jnp.zeros((ENC, KEYS), jnp.bfloat16)
            ids[0] = jnp.zeros((2, KEYS), jnp.int32)

        pad((0, 1))

    def out_copies(col, out_col):
        found = []
        for n, (buf, out) in enumerate(((attbuf, att_hbm), (grbuf, gr_hbm))):
            src = buf.at[his_rows, col]
            found.append(remote(src, out.at[:, out_col], out_send.at[n], out_recv.at[n], sibling))
            found.append(pltpu.make_async_copy(buf.at[rows, col], out.at[:, out_col], out_sem.at[n]))
        return found

    def columns(step, head, of_core):
        forth = jnp.where(jnp.logical_or(step == 0, step == 7), lax.div(step, 7) * 4, 0)
        for i in range(1, 7):
            forth = jnp.where(step == i, ROWS[i] * turn, forth)
        yy = lax.rem(y + forth + 8, 8)
        hh = yy * 2 + head
        return hh, pl.ds(pl.multiple_of(hh * HD, HD), HD), head_columns(head, yy, of_core)

    arrivals = (
        (
            lambda: None,
            lambda: (y_ring(3), x_pass_on(3, 4)),
            lambda: (y_ring(4), x_pass_on(5, 6)),
            lambda: x_pass_on(7),
        ),
        (
            lambda: None,
            lambda: y_arrived(0, 2),
            lambda: y_arrived(1, 2),
            lambda: y_arrived(0, 3),
            lambda: y_arrived(1, 3),
        ),
    )

    def work(step, carry):
        for c in range(2):
            for k, pass_on in enumerate(arrivals[c]):
                pl.when(jnp.logical_and(step == k, core == c))(lambda pass_on=pass_on: pass_on() and None)

        pl.when(jnp.logical_and(step == 0, z_hi == 1))(prev_arrived)
        turn_of = step - z_hi

        @pl.when(jnp.logical_and(turn_of >= 0, turn_of < 8))
        def _():
            attend(turn_of)

        return carry

    def attend(step):
        pl.when(step == 0)(prev_whole)
        for i in range(8):
            pl.when(jnp.logical_and(step == i, core == 0))(lambda i=i: x_passed(i))

        @pl.when(jnp.logical_and(step == 7, core == 1))
        def _():
            y_arrived(0, 4)
            y_arrived(1, 4)

        first = columns(step, 0, core)[0]
        cols = [columns(step, h, core)[1] for h in range(2)]
        wt = w[pl.ds(first, 2)].reshape(2 * HD, 2 * ENC)
        kb[...] = dot(e1[...], wt[:, 0:512], NT).astype(jnp.bfloat16)
        vb[...] = dot(e2[...], wt[:, 384:896], NT).astype(jnp.bfloat16)
        for h in range(2):
            hs = slice(h * HD, h * HD + HD)
            for g, (r, m) in enumerate(GROUP_ROWS):
                ks = slice(KEYS * g, KEYS * g + KEYS)
                sbuf[h, r:r + m] = dot(qs[r:r + m, cols[h]], kb[ks, hs], NT)
                dbuf[h, r:r + m] = dot(cts[r:r + m, cols[h]], vb[ks, hs], NT)
        for h in range(2):
            for g, (r, m) in enumerate(GROUP_ROWS):
                bias = jnp.where(ids[(g + 1) // 2, (g + 1) % 2:(g + 1) % 2 + 1, :] != 0, 0.0, MASKED)
                for c0 in range(r, r + m, CHUNK):
                    c1 = min(c0 + CHUNK, r + m)
                    pbuf[h, c0:c1], dsbuf[h, c0:c1] = softmax_parts(sbuf[h, c0:c1], dbuf[h, c0:c1], bias)
        for h in range(2):
            hs = slice(h * HD, h * HD + HD)
            for buf, weights, other_side in ((attbuf, pbuf, vb), (grbuf, dsbuf, kb)):
                parts = [
                    dot(weights[h, r:r + m], other_side[KEYS * g:KEYS * g + KEYS, hs], NN)
                    for g, (r, m) in enumerate(GROUP_ROWS)
                ]
                moved = pltpu.roll(jnp.concatenate(parts, 0), SHIFTED - 1, 0)
                buf[:, cols[h]] = moved[0:256].astype(jnp.bfloat16)
        for h in range(2):
            _, col, out_col = columns(step, h, core)
            for copy in out_copies(col, out_col):
                copy.start()

    lax.fori_loop(0, 9, work, 0)

    for n, buf in enumerate((attbuf, grbuf)):
        pltpu.make_async_copy(buf.at[rows], buf.at[rows], out_sem.at[n]).wait()
        whole = remote(buf.at[rows], buf.at[rows], out_send.at[n], out_recv.at[n], sibling)
        whole.wait_send()
        whole.wait_recv()
    for n in range(2):
        whole_in(n, True).wait_send()
        sends[n + 2].wait_send()

    @pl.when(core == 0)
    def _():
        @pl.when(is_source)
        def _():
            for t in range(1, 4):
                z_copy(0, t, mine).wait_send()

        @pl.when(jnp.logical_not(is_source))
        def _():
            for t in range(1, 4):
                ensure("z", t)

        for r in range(2):
            for i in range(1, 7):
                ring_copy(r, i, y_side(i), abs(ROWS[i])).wait_send()
            for side in range(2):
                ring_copy(r, 0, side, 0).wait_send()

        for r in range(2):
            for i in range(8):
                for side in range(2):
                    along_x(r, i, side).wait_send()
                    x_forward(r, i, side)[1].wait_send()

    @pl.when(core == 1)
    def _():
        @pl.when(is_source)
        def _():
            for t in range(1, 4):
                z_copy(0, t, mine).wait_send()

        @pl.when(jnp.logical_not(is_source))
        def _():
            for t in range(1, 4):
                ensure("z", t)

        for r in range(2):
            for t in range(1, 4):
                x_copy(r, t).wait_send()
        for r in range(2):
            for j in range(4):
                for side in range(2):
                    for distance in range(4):
                        along_y(r, j, side, distance).wait_send()

        @pl.when(z_hi == 0)
        def _():
            for copy in prev_copies():
                copy.wait_send()

    @pl.when(z_hi == 1)
    def _():
        prev_on().wait_send()


def hand_over(att_in, gr_in, att_out, gr_out, att_buf, gr_buf, in_sem, out_sem):
    arrays = ((att_in, att_buf, att_out), (gr_in, gr_buf, gr_out))
    parts = [(n, i, pl.ds(32 * i, 32)) for i in range(4) for n in range(2)]
    loads = [pltpu.make_async_copy(arrays[n][0].at[at], arrays[n][1].at[at], in_sem.at[n, i]) for n, i, at in parts]
    stores = [pltpu.make_async_copy(arrays[n][1].at[at], arrays[n][2].at[at], out_sem.at[n, i]) for n, i, at in parts]
    for load in loads:
        load.start()
    for load, store in zip(loads, stores):
        load.wait()
        store.start()
    for store in stores:
        store.wait()


def on_device(queries, encodings, neighbour_ids, w_key, w_value, cotangent):
    bf16, f32, dma = jnp.bfloat16, jnp.float32, pltpu.SemaphoreType.DMA
    whole, anywhere = pl.BlockSpec(memory_space=pltpu.VMEM), pl.BlockSpec(memory_space=pl.ANY)
    attended, query_grad = pl.pallas_call(
        kernel,
        out_shape=(jax.ShapeDtypeStruct((128, WIDTH), bf16),) * 2,
        in_specs=[anywhere] * 4 + [whole] * 2,
        out_specs=(anywhere,) * 2,
        scratch_shapes=[
            pltpu.VMEM((16, 4, PIECE, 2 * ENC), bf16),
            pltpu.VMEM((256, HALF), bf16),
            pltpu.VMEM((256, HALF), bf16),
            pltpu.VMEM((SHIFTED, HALF), bf16),
            pltpu.VMEM((SHIFTED, HALF), bf16),
            pltpu.VMEM((GROUPS, ENC, KEYS), bf16),
            pltpu.VMEM((GROUPS * KEYS, 512), bf16),
            pltpu.VMEM((GROUPS * KEYS, 512), bf16),
            pltpu.VMEM((3, 2, KEYS), jnp.int32),
            pltpu.VMEM((GROUPS * KEYS, 2 * HD), bf16),
            pltpu.VMEM((GROUPS * KEYS, 2 * HD), bf16),
            pltpu.VMEM((2, SHIFTED, KEYS), f32),
            pltpu.VMEM((2, SHIFTED, KEYS), f32),
            pltpu.VMEM((2, SHIFTED, KEYS), bf16),
            pltpu.VMEM((2, SHIFTED, KEYS), bf16),
            pltpu.VMEM((256, HALF), bf16),
            pltpu.VMEM((256, HALF), bf16),
            pltpu.SemaphoreType.REGULAR((15,)),
            dma((4,)), dma((4,)), dma((4,)),
            dma((5,)), dma((3,)),
            dma((16,)), dma((16,)),
            dma((24,)), dma((16,)),
            dma((64,)), dma((64,)),
            dma((2,)), dma((2,)), dma((2,)),
        ],
        compiler_params=pltpu.CompilerParams(
            collective_id=0, has_side_effects=True, vmem_limit_bytes=60 << 20
        ),
    )(queries, cotangent, jnp.swapaxes(encodings, 2, 3), neighbour_ids, w_key.T, w_value.T)
    attended, query_grad = pl.pallas_call(
        hand_over,
        out_shape=(jax.ShapeDtypeStruct((128, WIDTH), bf16),) * 2,
        in_specs=[anywhere] * 2,
        out_specs=(anywhere,) * 2,
        scratch_shapes=[pltpu.VMEM((128, WIDTH), bf16)] * 2 + [dma((2, 4)), dma((2, 4))],
    )(attended, query_grad)
    return attended[None], query_grad[None]


def solution(mesh):
    return jax.shard_map(
        on_device,
        mesh=mesh,
        in_specs=(
            P("dp", "seq", None),
            P("dp", "seq", None, None),
            P("dp", "seq", None),
            P(None, "dp"),
            P(None, "dp"),
            P("dp", "seq", None),
        ),
        out_specs=(P("dp", "seq", None), P("dp", "seq", None)),
        check_vma=False,
    )
```

```python
import jax
import jax.numpy as jnp
from jax import lax
from jax.experimental import pallas as pl
from jax.experimental.pallas import tpu as pltpu
from jax.sharding import PartitionSpec as P

HD = 128
ENC = 448
BLOCK = 64
KEYS = 256
WIDTH = 4096
HALF = WIDTH // 2
PIECE = 32
GROUPS = 5
SHIFTED = 272
FACTOR = HD ** -0.5
EXPONENT = FACTOR * 1.4426950408889634
MASKED = -1e30
NT = (((1,), (1,)), ((), ()))
NN = (((1,), (0,)), ((), ()))
TN = (((0,), (0,)), ((), ()))
MESH = pl.DeviceIdType.MESH
GROUP_ROWS = tuple((BLOCK * g, BLOCK if g < 4 else 16) for g in range(GROUPS))
CHUNK = 32

ROWS = (0, 1, -1, -2, 2, 3, -3, 4)


def dot(a, b, dims):
    return lax.dot_general(a, b, dims, preferred_element_type=jnp.float32)


def pick(core, first, second):
    return first + core * (second - first)


def softmax_parts(s, dp, bias):
    s = s + bias
    top = jnp.max(s, axis=1, keepdims=True)
    e = jnp.exp2((s - top) * EXPONENT)
    p = e * (1.0 / jnp.sum(e, axis=1, keepdims=True))
    rowdot = jnp.sum(p * dp, axis=1, keepdims=True)
    return p.astype(jnp.bfloat16), ((p * FACTOR) * (dp - rowdot)).astype(jnp.bfloat16)


def kernel(
    q_hbm, ct_hbm, e_hbm, ids_hbm, wk_ref, wv_ref, att_hbm, gr_hbm,
    w, qraw, ctraw, qs, cts, eraw, e1, e2, ids, kb, vb, sbuf, dbuf, pbuf, dsbuf, attbuf, grbuf,
    ready, in_sem, in_send, in_recv, prev_send, prev_recv, first_send, first_recv, z_send, z_recv,
    last_send, last_recv, out_sem, out_send, out_recv,
):
    dp, seq = lax.axis_index("dp"), lax.axis_index("seq")
    y, zl, x = lax.div(dp, 16), lax.rem(lax.div(dp, 4), 4), lax.rem(dp, 4)
    z_hi, core = lax.div(seq, 2), lax.rem(seq, 2)
    other = 1 - core
    zi_me = lax.div(zl, 2)
    is_source = lax.rem(zl, 2) == core
    turn = 1 - 2 * lax.rem(y, 2)
    z = z_hi * 4 + zl
    barrier = pltpu.get_barrier_semaphore()

    def place(axis, t):
        yy = lax.rem(y + t, 8) if axis == "y" else y
        zz = z_hi * 4 + lax.rem(zl + t, 4) if axis == "z" else z
        xx = lax.rem(x + t, 4) if axis == "x" else x
        return yy, zz, xx

    def peer(axis, t):
        yy, zz, xx = place(axis, t)
        return (yy * 16 + lax.rem(zz, 4) * 4 + xx, lax.div(zz, 4) * 2 + core)

    def rank(axis, yy, zz, xx):
        key = {"y": jnp.where(yy < 4, yy, 11 - yy), "x": jnp.where(xx < 2, xx, 5 - xx)}.get(axis, zz)
        return jnp.where(yy + zz + xx == 0, 99, key)

    def later(axis, t):
        return rank(axis, *place(axis, t)) > rank(axis, y, z, x)

    def slot(axis, t):
        return {"y": 0, "x": 7, "z": 10}[axis] + t - 1

    sizes = {"y": 8, "x": 4, "z": 4}
    sibling = (dp, z_hi * 2 + other)

    edges = [("z", t, True) for t in range(1, 4)] + [("x", t, True) for t in (1, 3)] + [("x", 2, core == 1)]
    edges += [("y", t, True) for t in (1, 7)]
    gives_prev = jnp.logical_and(z_hi == 0, core == 1)
    count = 1 + jnp.where(z_hi == 1, 1, 0)

    for axis, t, active in edges:
        after = jnp.logical_and(active, later(axis, t))
        before = jnp.logical_and(active, jnp.logical_not(later(axis, t)))
        count = count + jnp.where(before, 1, 0)

        @pl.when(after)
        def _():
            pl.semaphore_signal(barrier, inc=1, device_id=peer(axis, t), device_id_type=MESH)

    pl.semaphore_signal(barrier, inc=1, device_id=sibling, device_id_type=MESH)

    @pl.when(gives_prev)
    def _():
        for t in range(2):
            pl.semaphore_signal(barrier, inc=1, device_id=(dp, 2 + t), device_id_type=MESH)

    r0 = lax.broadcasted_iota(jnp.int32, (ENC, 512), 0)
    r1 = lax.broadcasted_iota(jnp.int32, (ENC, 512), 1)
    place1 = (r0 == r1).astype(jnp.float32).astype(jnp.bfloat16)
    place2 = (r0 + (512 - ENC) == r1).astype(jnp.float32).astype(jnp.bfloat16)
    left = dot(wk_ref[...], place1, NN)
    right = dot(wv_ref[...], place2, NN)

    def piece(zi, yy, xx):
        return w.at[lax.rem(yy + 16, 8) * 2 + zi, lax.rem(xx + 8, 4)]

    mine = piece(zi_me, y, x)

    @pl.when(is_source)
    def _():
        mine[:, 0:384] = left[:, 0:384].astype(jnp.bfloat16)
        mine[:, 384:512] = (left[:, 384:512] + right[:, 0:128]).astype(jnp.bfloat16)
        mine[:, 512:896] = right[:, 128:512].astype(jnp.bfloat16)

    def remote(src, dst, send, recv, to):
        return pltpu.make_async_remote_copy(
            src_ref=src, dst_ref=dst, send_sem=send, recv_sem=recv, device_id=to, device_id_type=MESH
        )

    pl.semaphore_wait(barrier, count)

    for axis, t, active in edges:
        before = jnp.logical_and(active, jnp.logical_not(later(axis, t)))

        @pl.when(before)
        def _():
            pl.semaphore_signal(
                ready.at[slot(axis, sizes[axis] - t)], inc=1, device_id=peer(axis, t), device_id_type=MESH
            )

    @pl.when(z_hi == 1)
    def _():
        pl.semaphore_signal(ready.at[13 + core], inc=1, device_id=(dp, 1), device_id_type=MESH)

    def ensure(axis, t):
        @pl.when(later(axis, t))
        def _():
            pl.semaphore_wait(ready.at[slot(axis, t)], 1)

    def z_copy(i, t, here):
        return remote(here, here, z_send.at[i * 3 + t - 1], z_recv.at[zi_me * 8 + i], peer("z", t))

    def z_wait(zi, i, there):
        remote(there, there, z_send.at[0], z_recv.at[zi * 8 + i], peer("z", 1)).wait_recv()

    rows = pl.ds(pl.multiple_of(core * 128, 128), 128)
    his_rows = pl.ds(pl.multiple_of(other * 128, 128), 128)

    def head_columns(zi, yy, of_core):
        return pl.ds(pl.multiple_of((yy * 4 + zi * 2 + of_core) * HD, HD), HD)

    mine_e, his_e = eraw.at[pl.ds(1 + 2 * core, 2)], eraw.at[pl.ds(1 + 2 * other, 2)]

    def whole_in(n, send_part):
        buf = (qraw, ctraw)[n]
        part = buf.at[rows if send_part else his_rows]
        return remote(part, part, in_send.at[n], in_recv.at[n], sibling)

    def exchange(n):
        src, dst = (q_hbm, qraw)[0:2] if n == 0 else (ct_hbm, ctraw)

        def body(j, carry):
            yy, zi = lax.div(j, 2), lax.rem(j, 2)
            to = dst.at[rows, pl.ds(pl.multiple_of(j * HD, HD), HD)]
            pltpu.make_async_copy(src.at[0, :, head_columns(zi, yy, core)], to, in_sem.at[n]).start()
            remote(src.at[0, :, head_columns(zi, yy, other)], to, in_send.at[n], in_recv.at[n], sibling).start()
            return carry

        lax.fori_loop(0, 16, body, 0)

    locals_ = {
        2: pltpu.make_async_copy(e_hbm.at[0], mine_e, in_sem.at[2]),
        3: pltpu.make_async_copy(ids_hbm.at[0], ids.at[1 + core], in_sem.at[3]),
    }
    sends = {
        2: remote(e_hbm.at[0], mine_e, in_send.at[2], in_recv.at[2], sibling),
        3: remote(ids_hbm.at[0], ids.at[1 + core], in_send.at[3], in_recv.at[3], sibling),
    }
    exchange(0)
    exchange(1)
    for n in (2, 3):
        locals_[n].start()
        sends[n].start()

    def in_wait(n):
        if n < 2:
            buf = (qraw, ctraw)[n]
            pltpu.make_async_copy(buf.at[rows], buf.at[rows], in_sem.at[n]).wait()
            whole_in(n, False).wait_recv()
        else:
            locals_[n].wait()
            to = his_e if n == 2 else ids.at[1 + other]
            remote(to, to, in_send.at[n], in_recv.at[n], sibling).wait_recv()

    def shift(n):
        raw, out = ((qraw, qs), (ctraw, cts))[n]
        in_wait(n)

        def body(j, carry):
            cols = pl.ds(pl.multiple_of(j * 256, 256), 256)
            moved = pltpu.roll(raw[:, cols].astype(jnp.float32), 1, 0).astype(jnp.bfloat16)
            out[0:256, cols] = moved
            out[256:272, cols] = moved[0:16]
            return carry

        lax.fori_loop(0, 8, body, 0)

    def pad(slots):
        def body(n, carry):
            block = eraw[n]
            at = pl.ds(pl.multiple_of(n * KEYS, KEYS), KEYS)
            e1[at, :] = dot(block, place1, TN).astype(jnp.bfloat16)
            e2[at, :] = dot(block, place2, TN).astype(jnp.bfloat16)
            return carry

        lax.fori_loop(slots[0], slots[1], body, 0)

    def prepare(n):
        if n < 2:
            shift(n)
        elif n == 2:
            in_wait(2)
            in_wait(3)
            pad((1, 3))
        elif n == 3:
            pad((3, 5))

    def zi_of(r):
        return zi_me if r == 0 else 1 - zi_me

    def row(i):
        return y + (4 if ROWS[i] == 4 else ROWS[i] * turn) + 8

    def along_x(r, i, side):
        here = piece(zi_of(r), row(i), x)
        at = side * 16 + r * 8 + i
        return remote(here, here, last_send.at[0], last_recv.at[at], peer("x", 1 if side == 0 else 3))

    def x_forward(r, i, side):
        there = piece(zi_of(r), row(i), x + (3 if side == 0 else 1))
        half = there.at[pl.ds(16 * side, 16)]
        copy = remote(half, half, last_send.at[0], last_recv.at[32 + i], peer("x", 1 if side == 0 else 3))
        return there, copy

    def x_pass_on(*numbers):
        for i, r in ((i, r) for i in numbers for r in range(2)):
            for side in range(2):
                there, copy = x_forward(r, i, side)
                at = side * 16 + r * 8 + i
                remote(there, there, last_send.at[0], last_recv.at[at], peer("x", 1)).wait_recv()
                copy.start()

    def x_passed(i):
        there = w.at[pl.ds(lax.rem(row(i), 8) * 2, 2), lax.rem(x + 2, 4)]
        remote(there, there, last_send.at[0], last_recv.at[32 + i], peer("x", 1)).wait_recv()

    def y_side(i):
        return lax.div(1 + turn, 2) if ROWS[i] > 0 else lax.div(1 - turn, 2)

    def ring_copy(r, i, side, distance):
        here = piece(zi_of(r), row(i), x)
        if distance == 3:
            here = here.at[pl.ds(pl.multiple_of(16 * side, 16), 16)]
        at = side * 8 + distance * 2 + r
        t = 1 + 6 * side
        yy = lax.rem(y + t, 8)
        return remote(here, here, first_send.at[at], first_recv.at[at], (yy * 16 + zl * 4 + x, seq))

    def ring_wait(r, i, side, distance):
        there = piece(zi_of(r), row(i), x)
        if distance == 4:
            there = there.at[pl.ds(16 * side, 16)]
        at = side * 8 + (distance - 1) * 2 + r
        remote(there, there, first_send.at[0], first_recv.at[at], peer("y", 1)).wait_recv()

    def z_phase(forward):
        def to_later(t):
            @pl.when(jnp.logical_and(is_source, later("z", t)))
            def _():
                pl.semaphore_wait(ready.at[slot("z", t)], 1)
                z_copy(0, t, mine).start()

        for t in (1, 2, 3):
            @pl.when(jnp.logical_and(is_source, jnp.logical_not(later("z", t))))
            def _():
                z_copy(0, t, mine).start()

        to_later(1)
        to_later(2)
        pl.when(jnp.logical_not(is_source))(lambda: z_wait(zi_me, 0, mine))
        forward(0)
        to_later(3)
        z_wait(1 - zi_me, 0, piece(1 - zi_me, y, x))
        forward(1)

    def z_forward(r):
        for side in range(2):
            if r == 0:
                ensure("y", 1 + 6 * side)
                ensure("x", 1 + 2 * side)
            ring_copy(r, 0, side, 0).start()
            along_x(r, 0, side).start()

    def y_ring(distance):
        for i in range(1, 8):
            if abs(ROWS[i]) != distance:
                continue
            for r in range(2):
                if distance == 4:
                    ring_wait(r, i, 0, 4)
                    ring_wait(r, i, 1, 4)
                else:
                    ring_wait(r, i, y_side(i), distance)
                    ring_copy(r, i, y_side(i), distance).start()
                for side in range(2):
                    along_x(r, i, side).start()

    def along_y(r, j, side, distance):
        there = piece(zi_of(r), y + (8 - distance if side == 0 else distance) + 8, x + j)
        if distance == 3:
            there = there.at[pl.ds(16 * side, 16)]
        at = 24 if distance == 3 else side * 32 + distance * 8 + r * 4 + j
        return remote(there, there, last_send.at[0], last_recv.at[at], peer("y", 1 if side == 0 else 7))

    def y_arrived(r, distance):
        for j in range(4):
            for side in range(2):
                there = piece(zi_of(r), y + (8 - distance if side == 0 else distance) + 8, x + j)
                at = side * 32 + (distance - 1) * 8 + r * 4 + j
                remote(there, there, last_send.at[0], last_recv.at[at], peer("y", 1)).wait_recv()
                along_y(r, j, side, distance).start()

    def y_far():
        there = w.at[pl.ds(lax.rem(y + 4, 8) * 2, 2)]
        remote(there, there, last_send.at[0], last_recv.at[24], peer("y", 1)).wait_recv()

    def x_copy(r, t):
        here = piece(zi_of(r), y, x)
        return remote(here, here, first_send.at[r * 3 + t - 1], first_recv.at[r * 3 + 3 - t], peer("x", t))

    def x_forward_first(r):
        for t in (2, 1, 3):
            if r == 0:
                ensure("x", t)
            x_copy(r, t).start()
        for side in range(2):
            if r == 0:
                ensure("y", 1 + 6 * side)
            along_y(r, 0, side, 0).start()

    def x_phase(r):
        for j in (1, 3, 2):
            there = piece(zi_of(r), y, x + j)
            remote(there, there, first_send.at[0], first_recv.at[r * 3 + j - 1], peer("x", 1)).wait_recv()
            for side in range(2):
                along_y(r, j, side, 0).start()

    def prev_copies():
        return [
            remote(
                e_hbm.at[0, 1, pl.ds(224 * t, 224)], eraw.at[0, pl.ds(224 * t, 224)],
                prev_send.at[t], prev_recv.at[0], (dp, 2 + t),
            )
            for t in range(2)
        ] + [
            remote(ids_hbm.at[0], ids.at[0], prev_send.at[2 + t], prev_recv.at[1], (dp, 2 + t)) for t in range(2)
        ]

    @pl.when(core == 0)
    def _():
        z_phase(z_forward)
        prepare(0)
        y_ring(1)
        prepare(1)
        x_pass_on(0)
        prepare(2)
        y_ring(2)
        prepare(3)
        x_pass_on(1, 2)

    @pl.when(core == 1)
    def _():
        z_phase(x_forward_first)
        prepare(0)
        x_phase(0)
        x_phase(1)
        for n in range(1, 4):
            prepare(n)

        @pl.when(z_hi == 0)
        def _():
            for t in range(2):
                pl.semaphore_wait(ready.at[13 + t], 1)
            for copy in prev_copies():
                copy.start()

        y_arrived(0, 1)
        y_arrived(1, 1)

    def prev_on():
        half = eraw.at[0, pl.ds(pl.multiple_of(core * 224, 32), 224)]
        return remote(half, half, prev_send.at[4], prev_recv.at[2], sibling)

    def prev_arrived():
        half = eraw.at[0, pl.ds(pl.multiple_of(core * 224, 32), 224)]
        remote(half, half, prev_send.at[0], prev_recv.at[0], sibling).wait_recv()
        remote(ids.at[0], ids.at[0], prev_send.at[2], prev_recv.at[1], sibling).wait_recv()
        prev_on().start()

    def prev_whole():
        @pl.when(z_hi == 1)
        def _():
            half = eraw.at[0, pl.ds(pl.multiple_of(other * 224, 32), 224)]
            remote(half, half, prev_send.at[4], prev_recv.at[2], sibling).wait_recv()

        @pl.when(z_hi == 0)
        def _():
            eraw[0] = jnp.zeros((ENC, KEYS), jnp.bfloat16)
            ids[0] = jnp.zeros((2, KEYS), jnp.int32)

        pad((0, 1))

    def out_copies(col, out_col):
        found = []
        for n, (buf, out) in enumerate(((attbuf, att_hbm), (grbuf, gr_hbm))):
            src = buf.at[his_rows, col]
            found.append(remote(src, out.at[:, out_col], out_send.at[n], out_recv.at[n], sibling))
            found.append(pltpu.make_async_copy(buf.at[rows, col], out.at[:, out_col], out_sem.at[n]))
        return found

    def columns(step, head, of_core):
        forth = jnp.where(jnp.logical_or(step == 0, step == 7), lax.div(step, 7) * 4, 0)
        for i in range(1, 7):
            forth = jnp.where(step == i, ROWS[i] * turn, forth)
        yy = lax.rem(y + forth + 8, 8)
        hh = yy * 2 + head
        return hh, pl.ds(pl.multiple_of(hh * HD, HD), HD), head_columns(head, yy, of_core)

    arrivals = (
        (
            lambda: None,
            lambda: (y_ring(3), x_pass_on(3, 4)),
            lambda: (y_ring(4), x_pass_on(5, 6)),
            lambda: x_pass_on(7),
        ),
        (
            lambda: None,
            lambda: y_arrived(0, 2),
            lambda: y_arrived(1, 2),
            lambda: y_arrived(0, 3),
            lambda: y_arrived(1, 3),
        ),
    )

    def work(step, carry):
        for c in range(2):
            for k, pass_on in enumerate(arrivals[c]):
                pl.when(jnp.logical_and(step == k, core == c))(lambda pass_on=pass_on: pass_on() and None)

        pl.when(jnp.logical_and(step == 0, z_hi == 1))(prev_arrived)
        turn_of = step - z_hi

        @pl.when(jnp.logical_and(turn_of >= 0, turn_of < 8))
        def _():
            attend(turn_of)

        return carry

    def attend(step):
        pl.when(step == 0)(prev_whole)
        for i in range(8):
            pl.when(jnp.logical_and(step == i, core == 0))(lambda i=i: x_passed(i))

        @pl.when(jnp.logical_and(step == 7, core == 1))
        def _():
            y_far()

        first = columns(step, 0, core)[0]
        cols = [columns(step, h, core)[1] for h in range(2)]
        wt = w[pl.ds(first, 2)].reshape(2 * HD, 2 * ENC)
        kb[...] = dot(e1[...], wt[:, 0:512], NT).astype(jnp.bfloat16)
        vb[...] = dot(e2[...], wt[:, 384:896], NT).astype(jnp.bfloat16)
        for h in range(2):
            hs = slice(h * HD, h * HD + HD)
            for g, (r, m) in enumerate(GROUP_ROWS):
                ks = slice(KEYS * g, KEYS * g + KEYS)
                sbuf[h, r:r + m] = dot(qs[r:r + m, cols[h]], kb[ks, hs], NT)
                dbuf[h, r:r + m] = dot(cts[r:r + m, cols[h]], vb[ks, hs], NT)
        for h in range(2):
            for g, (r, m) in enumerate(GROUP_ROWS):
                bias = jnp.where(ids[(g + 1) // 2, (g + 1) % 2:(g + 1) % 2 + 1, :] != 0, 0.0, MASKED)
                for c0 in range(r, r + m, CHUNK):
                    c1 = min(c0 + CHUNK, r + m)
                    pbuf[h, c0:c1], dsbuf[h, c0:c1] = softmax_parts(sbuf[h, c0:c1], dbuf[h, c0:c1], bias)
        for h in range(2):
            hs = slice(h * HD, h * HD + HD)
            for buf, weights, other_side in ((attbuf, pbuf, vb), (grbuf, dsbuf, kb)):
                parts = [
                    dot(weights[h, r:r + m], other_side[KEYS * g:KEYS * g + KEYS, hs], NN)
                    for g, (r, m) in enumerate(GROUP_ROWS)
                ]
                moved = pltpu.roll(jnp.concatenate(parts, 0), SHIFTED - 1, 0)
                buf[:, cols[h]] = moved[0:256].astype(jnp.bfloat16)
        for h in range(2):
            _, col, out_col = columns(step, h, core)
            for copy in out_copies(col, out_col):
                copy.start()

    lax.fori_loop(0, 9, work, 0)

    for n, buf in enumerate((attbuf, grbuf)):
        pltpu.make_async_copy(buf.at[rows], buf.at[rows], out_sem.at[n]).wait()
        whole = remote(buf.at[rows], buf.at[rows], out_send.at[n], out_recv.at[n], sibling)
        whole.wait_send()
        whole.wait_recv()
    for n in range(2):
        whole_in(n, True).wait_send()
        sends[n + 2].wait_send()

    @pl.when(core == 0)
    def _():
        @pl.when(is_source)
        def _():
            for t in range(1, 4):
                z_copy(0, t, mine).wait_send()

        @pl.when(jnp.logical_not(is_source))
        def _():
            for t in range(1, 4):
                ensure("z", t)

        for r in range(2):
            for i in range(1, 7):
                ring_copy(r, i, y_side(i), abs(ROWS[i])).wait_send()
            for side in range(2):
                ring_copy(r, 0, side, 0).wait_send()

        sent = w.at[pl.ds(0, 12)]
        remote(sent, sent, last_send.at[0], last_recv.at[0], peer("x", 1)).wait_send()

    @pl.when(core == 1)
    def _():
        @pl.when(is_source)
        def _():
            for t in range(1, 4):
                z_copy(0, t, mine).wait_send()

        @pl.when(jnp.logical_not(is_source))
        def _():
            for t in range(1, 4):
                ensure("z", t)

        for r in range(2):
            for t in range(1, 4):
                x_copy(r, t).wait_send()
        sent = w.at[pl.ds(0, 14)]
        remote(sent, sent, last_send.at[0], last_recv.at[0], peer("y", 1)).wait_send()

        @pl.when(z_hi == 0)
        def _():
            for copy in prev_copies():
                copy.wait_send()

    @pl.when(z_hi == 1)
    def _():
        prev_on().wait_send()


def hand_over(att_in, gr_in, att_out, gr_out, att_buf, gr_buf, in_sem, out_sem):
    arrays = ((att_in, att_buf, att_out), (gr_in, gr_buf, gr_out))
    parts = [(n, i, pl.ds(32 * i, 32)) for i in range(4) for n in range(2)]
    loads = [pltpu.make_async_copy(arrays[n][0].at[at], arrays[n][1].at[at], in_sem.at[n, i]) for n, i, at in parts]
    stores = [pltpu.make_async_copy(arrays[n][1].at[at], arrays[n][2].at[at], out_sem.at[n, i]) for n, i, at in parts]
    for load in loads:
        load.start()
    for load, store in zip(loads, stores):
        load.wait()
        store.start()
    for store in stores:
        store.wait()


def on_device(queries, encodings, neighbour_ids, w_key, w_value, cotangent):
    bf16, f32, dma = jnp.bfloat16, jnp.float32, pltpu.SemaphoreType.DMA
    whole, anywhere = pl.BlockSpec(memory_space=pltpu.VMEM), pl.BlockSpec(memory_space=pl.ANY)
    attended, query_grad = pl.pallas_call(
        kernel,
        out_shape=(jax.ShapeDtypeStruct((128, WIDTH), bf16),) * 2,
        in_specs=[anywhere] * 4 + [whole] * 2,
        out_specs=(anywhere,) * 2,
        scratch_shapes=[
            pltpu.VMEM((16, 4, PIECE, 2 * ENC), bf16),
            pltpu.VMEM((256, HALF), bf16),
            pltpu.VMEM((256, HALF), bf16),
            pltpu.VMEM((SHIFTED, HALF), bf16),
            pltpu.VMEM((SHIFTED, HALF), bf16),
            pltpu.VMEM((GROUPS, ENC, KEYS), bf16),
            pltpu.VMEM((GROUPS * KEYS, 512), bf16),
            pltpu.VMEM((GROUPS * KEYS, 512), bf16),
            pltpu.VMEM((3, 2, KEYS), jnp.int32),
            pltpu.VMEM((GROUPS * KEYS, 2 * HD), bf16),
            pltpu.VMEM((GROUPS * KEYS, 2 * HD), bf16),
            pltpu.VMEM((2, SHIFTED, KEYS), f32),
            pltpu.VMEM((2, SHIFTED, KEYS), f32),
            pltpu.VMEM((2, SHIFTED, KEYS), bf16),
            pltpu.VMEM((2, SHIFTED, KEYS), bf16),
            pltpu.VMEM((256, HALF), bf16),
            pltpu.VMEM((256, HALF), bf16),
            pltpu.SemaphoreType.REGULAR((15,)),
            dma((4,)), dma((4,)), dma((4,)),
            dma((5,)), dma((3,)),
            dma((16,)), dma((16,)),
            dma((24,)), dma((16,)),
            dma((1,)), dma((64,)),
            dma((2,)), dma((2,)), dma((2,)),
        ],
        compiler_params=pltpu.CompilerParams(
            collective_id=0, has_side_effects=True, vmem_limit_bytes=60 << 20
        ),
    )(queries, cotangent, jnp.swapaxes(encodings, 2, 3), neighbour_ids, w_key.T, w_value.T)
    attended, query_grad = pl.pallas_call(
        hand_over,
        out_shape=(jax.ShapeDtypeStruct((128, WIDTH), bf16),) * 2,
        in_specs=[anywhere] * 2,
        out_specs=(anywhere,) * 2,
        scratch_shapes=[pltpu.VMEM((128, WIDTH), bf16)] * 2 + [dma((2, 4)), dma((2, 4))],
    )(attended, query_grad)
    return attended[None], query_grad[None]


def solution(mesh):
    return jax.shard_map(
        on_device,
        mesh=mesh,
        in_specs=(
            P("dp", "seq", None),
            P("dp", "seq", None, None),
            P("dp", "seq", None),
            P(None, "dp"),
            P(None, "dp"),
            P("dp", "seq", None),
        ),
        out_specs=(P("dp", "seq", None), P("dp", "seq", None)),
        check_vma=False,
    )
```
